512 devices in a mesh: aux: 4 (over x), blk: 128 (over z, y, core).
Axes of the slice: x: 4, y: 8, z: 8, core: 2. Of those that a mesh axis runs over, the one named last changes fastest.
Arguments:
- slabs: bfloat16 [32768, 128, 128], P('blk', 'aux'), may hold values from -0.75 to 0.75
- orbital_start: int32 [128], P('blk'), may hold values from 0 to 4095, as said below
- orbital_count: int32 [128], P('blk'), may hold values from 32 to 128
- partners: int32 [128, 4], P('blk'), may hold values from -1 to 127, as said below
- density: bfloat16 [128, 4, 256, 256], P('blk', None, 'aux'), may hold values from -6 to 6
- direction: bfloat16 [128, 4, 256, 256], P('blk', None, 'aux'), may hold values from -6 to 6
- step_lengths: float32 [3], replicated, may hold values from 0.1 to 1
Outputs:
- exchange_tiles: bfloat16 [128, 4, 256, 256], P('blk', None, 'aux')
- energies: float32 [3], replicated
The draws below stay inside these ranges and needn't reach their ends.
Inputs may be any that keep to these rules, and one draw needn't show every extreme that they name: orbital_start[i] lies in i * (32) to i * 32 + 128 // 4 - 1. Row i lists distinct partners j with i <= j <= i + 3 and j < 128 in ascending order, always i itself first, then -1 for the empty slots.
All inputs are finite; a program needn't handle non-finite values.
Results may differ from the reference program's by a relative error of at most 0.009.
Values may be sent and summed in bfloat16 or wider, within the bound.
No kernel may reach another device: no remote copies, remote signals or barrier semaphores. Data moves between devices by JAX's collectives and lax.ppermute only.
A program may use at most 64 MiB of HBM per device.

```python
import math
import jax
import jax.numpy as jnp
from jax import lax

BS = 256
W = 128
REACH = 3
PCAP = 4
NB = 128
NAO = 32768
NAUX = 128


def draw_orbital_start(key, part):
    key = jax.random.fold_in(key, 11)
    quarter = W // 4
    jitter = jax.random.randint(key, (NB,), 0, quarter)
    jitter = jitter.at[0].set(0).at[NB - 1].set(quarter - 1)
    return (jnp.arange(NB, dtype=jnp.int32) * quarter + jitter).astype(jnp.int32)


def draw_orbital_count(key, part):
    key = jax.random.fold_in(key, 23)
    counts = jax.random.randint(key, (NB,), W // 4, W + 1)
    counts = counts.at[0].set(W).at[1].set(W // 4)
    return counts.astype(jnp.int32)


def draw_partners(key, part):
    key = jax.random.fold_in(key, 37)
    picks = jax.random.randint(key, (NB, PCAP), 0, 2)
    picks = picks.at[:, 0].set(1).at[0, :].set(1)
    offsets = jnp.arange(PCAP, dtype=jnp.int32)[None, :]
    blocks = jnp.arange(NB, dtype=jnp.int32)[:, None]
    picked = (picks == 1) & (blocks + offsets < NB)
    order_key = jnp.where(picked, offsets, PCAP + offsets)
    order = jnp.argsort(order_key, axis=1, stable=True)
    sorted_offsets = jnp.take_along_axis(jnp.broadcast_to(offsets, (NB, PCAP)), order, axis=1)
    sorted_picked = jnp.take_along_axis(picked, order, axis=1)
    return jnp.where(sorted_picked, blocks + sorted_offsets, -1).astype(jnp.int32)


def level_of(rng, dims, split, least, top_value):
    factor_of = 1.0
    for position, parts in split:
        draws = jax.random.uniform(jax.random.fold_in(jax.random.fold_in(rng, 6), position), (parts,), jnp.float32, least / len(split), top_value / len(split))
        factor_of = factor_of * jnp.repeat(jnp.exp(draws), dims[position] // parts).reshape((-1,) + (1,) * (len(dims) - 1 - position))
    return factor_of


def centred(rng, extent, width, bound, shards=(), kind=jnp.bfloat16):
    drawn = jax.random.normal(rng, extent, jnp.float32) * width
    if len(shards) > 0:
        drawn = level_of(rng, extent, shards, -0.22, 0.18) * drawn
    return jnp.clip(drawn, min=-bound, max=bound).astype(kind)


def setup_inputs(seed: int = 0) -> dict:
    streams_of = jax.random.split(jax.random.key(seed), 8)
    return {
        "slabs": centred(streams_of[0], (NAO, NAUX, W), 0.125, 0.75, ((0, 128), (1, 4))),
        "orbital_start": draw_orbital_start(jax.random.fold_in(streams_of[7], 71), 0),
        "orbital_count": draw_orbital_count(jax.random.fold_in(streams_of[7], 71), 0),
        "partners": draw_partners(jax.random.fold_in(streams_of[7], 71), 0),
        "density": centred(streams_of[4], (NB, PCAP, BS, BS), 1.0, 6.0, ((0, 128), (2, 4))),
        "direction": centred(streams_of[5], (NB, PCAP, BS, BS), 1.0, 6.0, ((0, 128), (2, 4))),
        "step_lengths": jnp.clip(jnp.exp(jax.random.uniform(streams_of[6], (3,), jnp.float32, math.log(0.1), math.log(1.0))), 0.1, 1.0),
    }


def reference(slabs, orbital_start, orbital_count, partners, density, direction, step_lengths):
    blocks = slabs.reshape(NB, BS, NAUX, W)
    lanes = jnp.arange(W, dtype=jnp.int32)
    offsets = jnp.arange(REACH + 1, dtype=jnp.int32)

    def per_block(index):
        left = lax.dynamic_index_in_dim(blocks, index, 0, keepdims=False).reshape(BS, NAUX * W)
        start_i = lax.dynamic_index_in_dim(orbital_start, index, 0, keepdims=False)
        count_i = lax.dynamic_index_in_dim(orbital_count, index, 0, keepdims=False)
        tiles = []
        for offset in range(REACH + 1):
            other = index + offset
            inside = other < NB
            clamped = jnp.minimum(other, NB - 1).astype(jnp.int32)
            piece = lax.dynamic_index_in_dim(blocks, clamped, 0, keepdims=False)
            start_j = lax.dynamic_index_in_dim(orbital_start, clamped, 0, keepdims=False)
            count_j = jnp.where(inside, lax.dynamic_index_in_dim(orbital_count, clamped, 0, keepdims=False), 0)
            source = (start_i + lanes - start_j).astype(jnp.int32)
            usable = (source >= 0) & (source < count_j) & (lanes < count_i)
            taken = jnp.take(piece, jnp.clip(source, 0, W - 1), axis=2)
            moved = jnp.where(usable, taken, jnp.zeros((), jnp.bfloat16))
            tile = lax.dot_general(left, moved.reshape(BS, NAUX * W), (((1,), (1,)), ((), ())), preferred_element_type=jnp.float32)
            tiles.append(tile)
        stacked = jnp.stack(tiles)
        row = lax.dynamic_index_in_dim(partners, index, 0, keepdims=False)
        onehot = ((row[:, None] - index == offsets[None, :]) & (row[:, None] >= 0)).astype(jnp.float32)
        full = jnp.einsum('sk,kmn->smn', onehot, stacked)
        weight = jnp.where(row < 0, 0.0, jnp.where(row == index, 1.0, 2.0)).astype(jnp.float32)
        dens = lax.dynamic_index_in_dim(density, index, 0, keepdims=False).astype(jnp.float32)
        dirs = lax.dynamic_index_in_dim(direction, index, 0, keepdims=False).astype(jnp.float32)
        first = jnp.sum(weight * lax.optimization_barrier(jnp.sum(dens * full, axis=(1, 2))))
        second = jnp.sum(weight * lax.optimization_barrier(jnp.sum(dirs * full, axis=(1, 2))))
        return (full.astype(jnp.bfloat16), first, second)
    exchange_tiles, firsts, seconds = lax.map(per_block, jnp.arange(NB, dtype=jnp.int32))
    scale = 1.0 / (BS * math.sqrt(NB * PCAP))
    energies = -0.5 * (jnp.sum(firsts) + step_lengths * jnp.sum(seconds)) * scale
    return (exchange_tiles, energies.astype(jnp.float32))
```

```python
import functools
import math

import jax
import jax.numpy as jnp
from jax import lax
from jax.experimental import pallas as pl
from jax.experimental.pallas import tpu as pltpu
from jax.sharding import PartitionSpec as P

VMEM = pltpu.VMEM
SMEM = pltpu.SMEM
NT = (((1,), (1,)), ((), ()))
LIMIT = 40 * 1024 * 1024


def spec(space):
    return pl.BlockSpec(memory_space=space)


def moved_by(value, axis, steps):
    count = lax.axis_size(axis)
    pairs = [(source, source + steps) for source in range(count) if 0 <= source + steps < count]
    return lax.ppermute(value, axis, pairs)


def align_kernel(chunk, auxb, start_ref, count_ref, row_ref, slab_ref, high_ref, low_ref, wide_ref, packed_ref, select_ref):
    groups = auxb // 4

    @pl.when(pl.program_id(0) == 0)
    def _():
        shift = start_ref[0] - 32 * row_ref[0, 0]
        lane = lax.broadcasted_iota(jnp.int32, (512, 640), 0)
        out = lax.broadcasted_iota(jnp.int32, (512, 640), 1)
        a = lane & 127
        place = ((out >> 7) << 5) + (out & 31)
        same = (lane >> 7) == ((out & 127) >> 5)
        hit = same & (a + shift == place) & (a < count_ref[0])
        select_ref[...] = jnp.where(hit, 1.0, 0.0).astype(jnp.bfloat16)

    wide_ref[...] = slab_ref[...].astype(jnp.float32).reshape(chunk * auxb, 128)
    for p in range(auxb):
        g, m = divmod(p, 4)
        rows = wide_ref[pl.ds(p, chunk, stride=auxb), :]
        packed_ref[g * chunk:(g + 1) * chunk, m * 128:(m + 1) * 128] = rows.astype(jnp.bfloat16)
    placed = jnp.dot(packed_ref[...], select_ref[...], preferred_element_type=jnp.float32).astype(jnp.bfloat16)
    for g in range(groups):
        part = placed[g * chunk:(g + 1) * chunk]
        for q in range(5):
            piece = part[:, q * 128:(q + 1) * 128]
            if q >= 1:
                high_ref[q - 1, :, g * 128:(g + 1) * 128] = piece
            if q <= 2:
                low_ref[q, :, g * 128:(g + 1) * 128] = piece


def align(slabs, start, count, row):
    rows, auxb, _ = slabs.shape
    chunk = 64
    depth = auxb * 32
    groups = auxb // 4
    return pl.pallas_call(
        functools.partial(align_kernel, chunk, auxb),
        grid=(rows // chunk,),
        in_specs=[
            spec(SMEM),
            spec(SMEM),
            spec(SMEM),
            pl.BlockSpec((chunk, auxb, 128), lambda n: (n, 0, 0)),
        ],
        out_specs=[
            pl.BlockSpec((4, chunk, depth), lambda n: (0, n, 0)),
            pl.BlockSpec((3, chunk, depth), lambda n: (0, n, 0)),
        ],
        out_shape=[
            jax.ShapeDtypeStruct((4, rows, depth), jnp.bfloat16),
            jax.ShapeDtypeStruct((3, rows, depth), jnp.bfloat16),
        ],
        scratch_shapes=[
            VMEM((chunk * auxb, 128), jnp.float32),
            VMEM((groups * chunk, 512), jnp.bfloat16),
            VMEM((512, 640), jnp.bfloat16),
        ],
        compiler_params=pltpu.CompilerParams(vmem_limit_bytes=LIMIT),
    )(start, count, row, slabs)


def by_offset_kernel(row_ref, density_ref, direction_ref, even_ref, odd_ref):
    block = row_ref[0, 0]
    for k in range(4):
        out = even_ref if k % 2 == 0 else odd_ref
        for which, source in enumerate((density_ref, direction_ref)):
            total = jnp.zeros(source.shape[2:], jnp.float32)
            for s in range(4):
                other = row_ref[0, s]
                full = 1.0 if s == 0 else 2.0
                weight = jnp.where((other >= 0) & (other - block == k), full, 0.0)
                total = total + weight * source[0, s].astype(jnp.float32)
            out[k // 2, which] = total.astype(jnp.bfloat16)


def by_offset(row, density, direction):
    shape = jax.ShapeDtypeStruct((2, 2) + density.shape[2:], jnp.bfloat16)
    return pl.pallas_call(
        by_offset_kernel,
        in_specs=[spec(SMEM), spec(VMEM), spec(VMEM)],
        out_specs=[spec(VMEM), spec(VMEM)],
        out_shape=[shape, shape],
    )(row, density, direction)


def product(left, right):
    total = None
    for a, b in zip(left, right):
        term = lax.dot_general(a, b, NT, preferred_element_type=jnp.float32)
        total = term if total is None else total + term
    return total


def tile_sums(tile, k, weights_ref):
    parts = []
    for which in range(2):
        total = jnp.zeros((8, 256), jnp.float32)
        for source in range(4):
            piece = weights_ref[source, k, which].astype(jnp.float32) * tile[source * 64:(source + 1) * 64]
            total = total + jnp.sum(piece.reshape(8, 8, 256), axis=0)
        parts.append(total)
    return parts


def near_kernel(high_ref, low_ref, before_ref, weights_ref, out_ref, sums_ref):
    own = [low_ref[0]] + [high_ref[q] for q in range(4)]
    t0 = product(own, own)
    t1 = product([before_ref[q] for q in range(4)], own[:4])
    sums = [jnp.zeros((8, 256), jnp.float32)] * 2
    for k, tile in enumerate((t0, t1)):
        sums = [a + b for a, b in zip(sums, tile_sums(tile, k, weights_ref))]
        for to in range(4):
            out_ref[to, k] = tile[to * 64:(to + 1) * 64].astype(jnp.bfloat16)
    for which in range(2):
        sums_ref[which] = sums[which]


def far_kernel(high_ref, before_ref, after_ref, weights_ref, sums_in_ref, out_ref):
    t2 = product([high_ref[q + 1] for q in range(3)], [after_ref[q] for q in range(3)])
    t3 = product([before_ref[q + 2] for q in range(2)], [after_ref[q] for q in range(2)])
    sums = [sums_in_ref[0], sums_in_ref[1]]
    for n, tile in enumerate((t2, t3)):
        sums = [a + b for a, b in zip(sums, tile_sums(tile, n + 2, weights_ref))]
        for to in range(4):
            out_ref[to, n * 64:(n + 1) * 64] = tile[to * 64:(to + 1) * 64].astype(jnp.bfloat16)
    lines = []
    for total in sums:
        value = jnp.broadcast_to(jnp.sum(total, keepdims=True), (8, 256))
        high = value.astype(jnp.bfloat16).astype(jnp.float32)
        rest = value - high
        middle = rest.astype(jnp.bfloat16).astype(jnp.float32)
        lines.append((high, middle, rest - middle))
    line = lax.broadcasted_iota(jnp.int32, (16, 256), 0)
    block = jnp.zeros((16, 256), jnp.float32)
    for which in range(2):
        for part in range(3):
            twice = jnp.concatenate([lines[which][part]] * 2, axis=0)
            block = jnp.where(line == which * 3 + part, twice, block)
    for to in range(4):
        out_ref[to, 128:144] = block.astype(jnp.bfloat16)


def near_sum_kernel(parts_ref, own_ref, before_ref):
    for k, out in enumerate((own_ref, before_ref)):
        total = parts_ref[0, k].astype(jnp.float32)
        for source in range(1, 4):
            total = total + parts_ref[source, k].astype(jnp.float32)
        out[...] = total.astype(jnp.bfloat16)


def far_sum_kernel(parts_ref, own_ref, before_ref, energy_ref):
    for n, out in enumerate((own_ref, before_ref)):
        total = parts_ref[0, n * 64:(n + 1) * 64].astype(jnp.float32)
        for source in range(1, 4):
            total = total + parts_ref[source, n * 64:(n + 1) * 64].astype(jnp.float32)
        out[...] = total.astype(jnp.bfloat16)
    extra = parts_ref[0, 128:144].astype(jnp.float32)
    for source in range(1, 4):
        extra = extra + parts_ref[source, 128:144].astype(jnp.float32)
    first = extra[0:1] + extra[1:2] + extra[2:3]
    second = extra[3:4] + extra[4:5] + extra[5:6]
    lane = lax.broadcasted_iota(jnp.int32, (1, 128), 1)
    both = jnp.where(lane < 64, first[:, :128], second[:, :128])
    count = energy_ref.shape[0]
    energy_ref[...] = jnp.broadcast_to(both[None], (count, 1, 128))


def finish_kernel(scale, row_ref, steps_ref, t0_ref, t1_ref, t2_ref, t3_ref, energy_ref, tiles_ref, out_ref):
    block = row_ref[0, 0]
    tiles = [t0_ref, t1_ref, t2_ref, t3_ref]
    for s in range(4):
        other = row_ref[0, s]
        total = jnp.zeros(t0_ref.shape, jnp.float32)
        for k in range(4):
            chosen = (other >= 0) & (other - block == k)
            total = jnp.where(chosen, tiles[k][...].astype(jnp.float32), total)
        tiles_ref[0, s] = total.astype(jnp.bfloat16)
    total = jnp.sum(energy_ref[...], axis=0)
    first = total[0, 0]
    second = total[0, 64]
    for n in range(3):
        out_ref[n] = -0.5 * (first + steps_ref[n] * second) * scale


def body(slabs, orbital_start, orbital_count, partners, density, direction, step_lengths):
    rows = slabs.shape[0]
    aux = lax.axis_size("aux")
    blocks = lax.axis_size("blk")
    slots = partners.shape[1]
    part = rows // aux
    bf16 = jnp.bfloat16
    params = pltpu.CompilerParams(vmem_limit_bytes=LIMIT)

    high, low = align(slabs, orbital_start, orbital_count, partners)
    after = moved_by(low, "blk", -2)
    before = moved_by(high, "blk", 1)
    even, odd = by_offset(partners, density, direction)
    odd = moved_by(odd, "blk", 1)
    weights = jnp.stack([even[0], odd[0], even[1], odd[1]])
    weights = jnp.broadcast_to(weights[None], (aux,) + weights.shape)
    weights = lax.all_to_all(weights, "aux", 0, 0, tiled=True)

    near, sums = pl.pallas_call(
        near_kernel,
        in_specs=[spec(VMEM)] * 4,
        out_specs=[spec(VMEM)] * 2,
        out_shape=[
            jax.ShapeDtypeStruct((aux, 2, part, rows), bf16),
            jax.ShapeDtypeStruct((2, 8, rows), jnp.float32),
        ],
        compiler_params=params,
    )(high, low, before, weights)
    near = lax.all_to_all(near, "aux", 0, 0, tiled=True)
    tile = jax.ShapeDtypeStruct((part, rows), bf16)
    t0, t1 = pl.pallas_call(
        near_sum_kernel, in_specs=[spec(VMEM)], out_specs=[spec(VMEM)] * 2, out_shape=[tile, tile]
    )(near)
    t1 = moved_by(t1, "blk", -1)

    far = pl.pallas_call(
        far_kernel,
        in_specs=[spec(VMEM)] * 5,
        out_specs=spec(VMEM),
        out_shape=jax.ShapeDtypeStruct((aux, 2 * part + 16, rows), bf16),
        compiler_params=params,
    )(high, before, after, weights, sums)
    far = lax.all_to_all(far, "aux", 0, 0, tiled=True)
    t2, t3, energy = pl.pallas_call(
        far_sum_kernel,
        in_specs=[spec(VMEM)],
        out_specs=[spec(VMEM)] * 3,
        out_shape=[tile, tile, jax.ShapeDtypeStruct((blocks, 1, 128), jnp.float32)],
    )(far)
    t3 = moved_by(t3, "blk", -1)
    energy = lax.all_to_all(energy, "blk", 0, 0, tiled=True)

    scale = 1.0 / (rows * math.sqrt(blocks * slots))
    return pl.pallas_call(
        functools.partial(finish_kernel, scale),
        in_specs=[spec(SMEM)] * 2 + [spec(VMEM)] * 5,
        out_specs=[spec(VMEM), spec(SMEM)],
        out_shape=[
            jax.ShapeDtypeStruct((1, slots, part, rows), bf16),
            jax.ShapeDtypeStruct((3,), jnp.float32),
        ],
    )(partners, step_lengths, t0, t1, t2, t3, energy)


def solution(mesh):
    return jax.shard_map(
        body,
        mesh=mesh,
        in_specs=(
            P("blk", "aux", None),
            P("blk"),
            P("blk"),
            P("blk", None),
            P("blk", None, "aux", None),
            P("blk", None, "aux", None),
            P(),
        ),
        out_specs=(P("blk", None, "aux", None), P()),
        check_vma=False,
    )
```

```python
import functools
import math

import jax
import jax.numpy as jnp
from jax import lax
from jax.experimental import pallas as pl
from jax.experimental.pallas import tpu as pltpu
from jax.sharding import PartitionSpec as P

VMEM = pltpu.VMEM
SMEM = pltpu.SMEM
NT = (((1,), (1,)), ((), ()))
MIB = 1024 * 1024


def spec(space):
    return pl.BlockSpec(memory_space=space)


def moved_by(value, axis, steps):
    count = lax.axis_size(axis)
    pairs = [(source, source + steps) for source in range(count) if 0 <= source + steps < count]
    return lax.ppermute(value, axis, pairs)


def by_offset(row_ref, tiles_ref, even_ref, odd_ref):
    block = row_ref[0, 0]
    for k in range(4):
        out = even_ref if k % 2 == 0 else odd_ref
        for which in range(2):
            total = jnp.zeros(tiles_ref.shape[2:], jnp.float32)
            for s in range(4):
                other = row_ref[0, s]
                full = 1.0 if s == 0 else 2.0
                weight = jnp.where((other >= 0) & (other - block == k), full, 0.0)
                total = total + weight * tiles_ref[which, s].astype(jnp.float32)
            out[k // 2 * 2 + which] = total.astype(jnp.bfloat16)


def align_kernel(
    chunk,
    start_hbm,
    count_hbm,
    row_hbm,
    slab_hbm,
    density_hbm,
    direction_hbm,
    high_hbm,
    low_hbm,
    even_hbm,
    odd_hbm,
    start_ref,
    count_ref,
    row_ref,
    slab_ref,
    select_ref,
    high_ref,
    low_ref,
    tiles_ref,
    even_ref,
    odd_ref,
    small_sem,
    in_sem,
    out_sem,
    tile_sem,
):
    steps, _, auxb, _ = slab_ref.shape
    bf16 = jnp.bfloat16
    small = [
        pltpu.make_async_copy(source, target, small_sem.at[n])
        for n, (source, target) in enumerate(((start_hbm, start_ref), (count_hbm, count_ref), (row_hbm, row_ref)))
    ]
    loads = [
        pltpu.make_async_copy(slab_hbm.at[pl.ds(n * chunk, chunk)], slab_ref.at[n], in_sem.at[n]) for n in range(steps)
    ]
    tiles = [
        pltpu.make_async_copy(source.at[0], tiles_ref.at[n], tile_sem.at[n])
        for n, source in enumerate((density_hbm, direction_hbm))
    ]
    for copy in small + loads + tiles:
        copy.start()
    for copy in small:
        copy.wait()
    shift = start_ref[0] - 32 * row_ref[0, 0]
    count = count_ref[0]
    a = lax.broadcasted_iota(jnp.int32, (128, 256), 0)
    to = lax.broadcasted_iota(jnp.int32, (128, 256), 1)
    hit = (a < count) & (((a + shift) & 127) == ((to >> 6) << 5) + (to & 31))
    for m in range(2):
        select_ref[m * 128:(m + 1) * 128] = jnp.where(hit & (((to >> 5) & 1) == m), 1.0, 0.0).astype(bf16)
    first = (lax.broadcasted_iota(jnp.int32, (chunk, 128), 1) & 31) >= shift
    zero = jnp.zeros((chunk, 128), bf16)
    stores = []
    for n in range(steps):
        loads[n].wait()
        by_function = jnp.swapaxes(slab_ref[n], 0, 1)
        rows = slice(n * chunk, (n + 1) * chunk)
        for g in range(auxb // 4):
            parts = []
            for p in (4 * g, 4 * g + 2):
                pair = jnp.concatenate([by_function[p], by_function[p + 1]], axis=1)
                parts.append(jnp.dot(pair, select_ref[...], preferred_element_type=jnp.float32).astype(bf16))
            lanes = slice(g * 128, (g + 1) * 128)
            for q in range(4):
                piece = jnp.concatenate([part[:, q * 64:(q + 1) * 64] for part in parts], axis=1)
                if q == 0:
                    low_ref[0, rows, lanes] = jnp.where(first, piece, zero)
                    high_ref[3, rows, lanes] = jnp.where(first, zero, piece)
                    continue
                high_ref[q - 1, rows, lanes] = piece
                if q <= 2:
                    low_ref[q, rows, lanes] = piece
        for m, (source, target) in enumerate(((low_ref, low_hbm), (high_ref, high_hbm))):
            part = pl.ds(n * chunk, chunk)
            copy = pltpu.make_async_copy(source.at[:, part], target.at[:, part], out_sem.at[n, m])
            copy.start()
            stores.append(copy)
    for copy in tiles:
        copy.wait()
    by_offset(row_ref, tiles_ref, even_ref, odd_ref)
    targets = [even_hbm] + [odd_hbm.at[to] for to in range(4)]
    for n, target in enumerate(targets):
        copy = pltpu.make_async_copy(odd_ref if n else even_ref, target, tile_sem.at[2 + n])
        copy.start()
        stores.append(copy)
    for copy in stores:
        copy.wait()


def align(slabs, start, count, row, density, direction):
    rows, auxb, _ = slabs.shape
    chunk = 128
    steps = rows // chunk
    depth = auxb * 32
    high = (4, rows, depth)
    low = (3, rows, depth)
    tiles = (4,) + density.shape[2:]
    bf16 = jnp.bfloat16
    dma = pltpu.SemaphoreType.DMA
    return pl.pallas_call(
        functools.partial(align_kernel, chunk),
        in_specs=[spec(pl.ANY)] * 6,
        out_specs=[spec(pl.ANY)] * 4,
        out_shape=[jax.ShapeDtypeStruct(shape, bf16) for shape in (high, low, tiles, (4,) + tiles)],
        scratch_shapes=[
            SMEM((1,), jnp.int32),
            SMEM((1,), jnp.int32),
            SMEM(row.shape, jnp.int32),
            VMEM((steps, chunk, auxb, 128), bf16),
            VMEM((256, 256), bf16),
            VMEM(high, bf16),
            VMEM(low, bf16),
            VMEM((2,) + density.shape[1:], bf16),
            VMEM(tiles, bf16),
            VMEM(tiles, bf16),
            dma((3,)),
            dma((steps,)),
            dma((steps, 2)),
            dma((7,)),
        ],
        compiler_params=pltpu.CompilerParams(vmem_limit_bytes=60 * MIB),
    )(start, count, row, slabs, density, direction)


def product(left, right):
    total = None
    for a, b in zip(left, right):
        term = lax.dot_general(a, b, NT, preferred_element_type=jnp.float32)
        total = term if total is None else total + term
    return total


def tile_sums(tile, place, weights_ref):
    parts = []
    for which in range(2):
        total = jnp.zeros((8, 256), jnp.float32)
        for source in range(4):
            weight = weights_ref[source, place * 2 + which].astype(jnp.float32)
            piece = weight * tile[source * 64:(source + 1) * 64]
            total = total + jnp.sum(piece.reshape(8, 8, 256), axis=0)
        parts.append(total)
    return parts


def own_kernel(high_ref, low_ref, even_ref, tile_ref, out_ref):
    own = [low_ref[0]] + [high_ref[q] for q in range(4)]
    tile = product(own, own)
    tile_ref[...] = tile
    for to in range(4):
        out_ref[to, 0:4] = even_ref[...]
        out_ref[to, 4] = tile[to * 64:(to + 1) * 64].astype(jnp.bfloat16)


def near_kernel(high_ref, low_ref, before_ref, tile_ref, even_ref, out_ref, own_ref, sums_ref):
    own = [low_ref[0]] + [high_ref[q] for q in range(3)]
    out_ref[...] = product([before_ref[q] for q in range(4)], own)
    sums = tile_sums(tile_ref, 0, even_ref)
    for which in range(2):
        sums_ref[which] = sums[which]
    total = even_ref[0, 4].astype(jnp.float32)
    for source in range(1, 4):
        total = total + even_ref[source, 4].astype(jnp.float32)
    own_ref[...] = total.astype(jnp.bfloat16)


def far_kernel(high_ref, before_ref, after_ref, even_ref, odd_ref, near_ref, sums_in_ref, out_ref):
    t2 = product([high_ref[q + 1] for q in range(3)], [after_ref[q] for q in range(3)])
    t3 = product([before_ref[q + 2] for q in range(2)], [after_ref[q] for q in range(2)])
    sums = [sums_in_ref[0], sums_in_ref[1]]
    for tile, place, weights_ref in ((near_ref, 0, odd_ref), (t2, 1, even_ref), (t3, 1, odd_ref)):
        sums = [a + b for a, b in zip(sums, tile_sums(tile, place, weights_ref))]
    for to in range(4):
        part = slice(to * 64, (to + 1) * 64)
        for n, tile in enumerate((near_ref[part], t3[part], t2[part])):
            out_ref[to, n * 64:(n + 1) * 64] = tile.astype(jnp.bfloat16)
    lines = []
    for total in sums:
        value = jnp.broadcast_to(jnp.sum(total, keepdims=True), (8, 256))
        high = value.astype(jnp.bfloat16).astype(jnp.float32)
        rest = value - high
        middle = rest.astype(jnp.bfloat16).astype(jnp.float32)
        lines.append((high, middle, rest - middle))
    line = lax.broadcasted_iota(jnp.int32, (16, 256), 0)
    block = jnp.zeros((16, 256), jnp.float32)
    for which in range(2):
        for part in range(3):
            twice = jnp.concatenate([lines[which][part]] * 2, axis=0)
            block = jnp.where(line == which * 3 + part, twice, block)
    for to in range(4):
        out_ref[to, 192:208] = block.astype(jnp.bfloat16)


def sum_kernel(parts_ref, before_ref, own_ref, energy_ref):
    for n in range(3):
        rows = slice(n * 64, (n + 1) * 64)
        total = parts_ref[0, rows].astype(jnp.float32)
        for source in range(1, 4):
            total = total + parts_ref[source, rows].astype(jnp.float32)
        if n < 2:
            before_ref[n] = total.astype(jnp.bfloat16)
        else:
            own_ref[...] = total.astype(jnp.bfloat16)
    extra = parts_ref[0, 192:208].astype(jnp.float32)
    for source in range(1, 4):
        extra = extra + parts_ref[source, 192:208].astype(jnp.float32)
    first = extra[0:1] + extra[1:2] + extra[2:3]
    second = extra[3:4] + extra[4:5] + extra[5:6]
    lane = lax.broadcasted_iota(jnp.int32, (1, 128), 1)
    both = jnp.where(lane < 64, first[:, :128], second[:, :128])
    energy_ref[...] = jnp.broadcast_to(both[None], energy_ref.shape)


def energy_kernel(scale, steps_ref, energy_ref, out_ref):
    total = jnp.sum(energy_ref[...], axis=0)
    first = total[0, 0]
    second = total[0, 64]
    for n in range(3):
        out_ref[n] = -0.5 * (first + steps_ref[n] * second) * scale


def slot_kernel(row_ref, t0_ref, t2_ref, odd_ref, tiles_ref):
    block = row_ref[0, 0]
    tiles = [t0_ref[...], odd_ref[0], t2_ref[...], odd_ref[1]]
    for s in range(4):
        other = row_ref[0, s]
        total = jnp.zeros(t0_ref.shape, jnp.float32)
        for k in range(4):
            chosen = (other >= 0) & (other - block == k)
            total = jnp.where(chosen, tiles[k].astype(jnp.float32), total)
        tiles_ref[0, s] = total.astype(jnp.bfloat16)


def kernel_call(kernel, in_specs, out_shape, limit=16, out_specs=None):
    return pl.pallas_call(
        kernel,
        in_specs=in_specs,
        out_specs=out_specs or [spec(VMEM)] * len(out_shape),
        out_shape=out_shape,
        compiler_params=pltpu.CompilerParams(vmem_limit_bytes=limit * MIB),
    )


def body(slabs, orbital_start, orbital_count, partners, density, direction, step_lengths):
    rows = slabs.shape[0]
    aux = lax.axis_size("aux")
    blocks = lax.axis_size("blk")
    slots = partners.shape[1]
    part = rows // aux

    def half(*shape):
        return jax.ShapeDtypeStruct(shape, jnp.bfloat16)

    def single(*shape):
        return jax.ShapeDtypeStruct(shape, jnp.float32)

    high, low, even, odd = align(slabs, orbital_start, orbital_count, partners, density, direction)
    after = moved_by(low, "blk", -2)
    before = moved_by(high, "blk", 1)
    odd = lax.all_to_all(odd, "aux", 0, 0, tiled=True)
    odd = moved_by(odd, "blk", 1)

    t0, even = kernel_call(own_kernel, [spec(VMEM)] * 3, [single(rows, rows), half(aux, 5, part, rows)])(
        high, low, even
    )
    even = lax.all_to_all(even, "aux", 0, 0, tiled=True)
    t1, t0, sums = kernel_call(
        near_kernel, [spec(VMEM)] * 5, [single(rows, rows), half(part, rows), single(2, 8, rows)]
    )(high, low, before, t0, even)
    (far,) = kernel_call(far_kernel, [spec(VMEM)] * 7, [half(aux, 3 * part + 16, rows)])(
        high, before, after, even, odd, t1, sums
    )
    far = lax.all_to_all(far, "aux", 0, 0, tiled=True)
    odd, t2, energy = kernel_call(
        sum_kernel, [spec(VMEM)], [half(2, part, rows), half(part, rows), single(blocks, 1, 128)]
    )(far)
    odd = moved_by(odd, "blk", -1)
    energy = lax.all_to_all(energy, "blk", 0, 0, tiled=True)

    scale = 1.0 / (rows * math.sqrt(blocks * slots))
    (energies,) = kernel_call(
        functools.partial(energy_kernel, scale),
        [spec(SMEM), spec(VMEM)],
        [single(3)],
        out_specs=[spec(SMEM)],
    )(step_lengths, energy)
    t2, energies = lax.optimization_barrier((t2, energies))
    (tiles,) = kernel_call(
        slot_kernel, [spec(SMEM)] + [spec(VMEM)] * 3, [half(1, slots, part, rows)]
    )(partners, t0, t2, odd)
    return tiles, energies


def solution(mesh):
    return jax.shard_map(
        body,
        mesh=mesh,
        in_specs=(
            P("blk", "aux", None),
            P("blk"),
            P("blk"),
            P("blk", None),
            P("blk", None, "aux", None),
            P("blk", None, "aux", None),
            P(),
        ),
        out_specs=(P("blk", None, "aux", None), P()),
        check_vma=False,
    )
```

```python
import functools
import math

import jax
import jax.numpy as jnp
from jax import lax
from jax.experimental import pallas as pl
from jax.experimental.pallas import tpu as pltpu
from jax.sharding import PartitionSpec as P

VMEM = pltpu.VMEM
SMEM = pltpu.SMEM
NT = (((1,), (1,)), ((), ()))
MIB = 1024 * 1024
CHUNKS = (64, 128, 64)


def spec(space):
    return pl.BlockSpec(memory_space=space)


def moved_by(value, axis, steps):
    count = lax.axis_size(axis)
    pairs = [(source, source + steps) for source in range(count) if 0 <= source + steps < count]
    return lax.ppermute(value, axis, pairs)


def by_offset(row_ref, tiles_ref, even_ref, odd_ref):
    block = row_ref[0, 0]
    for k in range(4):
        out = even_ref if k % 2 == 0 else odd_ref
        for which in range(2):
            total = jnp.zeros(tiles_ref.shape[2:], jnp.float32)
            for s in range(4):
                other = row_ref[0, s]
                full = 1.0 if s == 0 else 2.0
                weight = jnp.where((other >= 0) & (other - block == k), full, 0.0)
                total = total + weight * tiles_ref[which, s].astype(jnp.float32)
            out[k // 2 * 2 + which] = total.astype(jnp.bfloat16)


def align_kernel(
    chunks,
    start_hbm,
    count_hbm,
    row_hbm,
    slab_hbm,
    density_hbm,
    direction_hbm,
    high_hbm,
    low_hbm,
    even_hbm,
    odd_hbm,
    start_ref,
    count_ref,
    row_ref,
    slab_ref,
    select_ref,
    high_ref,
    low_ref,
    tiles_ref,
    even_ref,
    odd_ref,
    small_sem,
    in_sem,
    out_sem,
    tile_sem,
):
    _, auxb, _ = slab_ref.shape
    begins = [sum(chunks[:n]) for n in range(len(chunks))]
    bf16 = jnp.bfloat16
    small = [
        pltpu.make_async_copy(source, target, small_sem.at[n])
        for n, (source, target) in enumerate(((start_hbm, start_ref), (count_hbm, count_ref), (row_hbm, row_ref)))
    ]
    loads = [
        pltpu.make_async_copy(slab_hbm.at[pl.ds(begin, chunk)], slab_ref.at[pl.ds(begin, chunk)], in_sem.at[n])
        for n, (begin, chunk) in enumerate(zip(begins, chunks))
    ]
    tiles = [
        pltpu.make_async_copy(source.at[0], tiles_ref.at[n], tile_sem.at[n])
        for n, source in enumerate((density_hbm, direction_hbm))
    ]
    for copy in small + loads + tiles:
        copy.start()
    for copy in small:
        copy.wait()
    shift = start_ref[0, 0] - 32 * row_ref[0, 0]
    count = count_ref[0, 0]
    a = lax.broadcasted_iota(jnp.int32, (128, 256), 0)
    to = lax.broadcasted_iota(jnp.int32, (128, 256), 1)
    hit = (a < count) & (((a + shift) & 127) == ((to >> 6) << 5) + (to & 31))
    for m in range(2):
        select_ref[m * 128:(m + 1) * 128] = jnp.where(hit & (((to >> 5) & 1) == m), 1.0, 0.0).astype(bf16)
    stores = []
    for n, (begin, chunk) in enumerate(zip(begins, chunks)):
        first = (lax.broadcasted_iota(jnp.int32, (chunk, 128), 1) & 31) >= shift
        zero = jnp.zeros((chunk, 128), bf16)
        loads[n].wait()
        rows = slice(begin, begin + chunk)
        by_function = jnp.swapaxes(slab_ref[rows], 0, 1)
        pairs = [jnp.concatenate([by_function[p], by_function[p + 1]], axis=1) for p in range(0, auxb, 2)]
        placed = jnp.dot(jnp.concatenate(pairs, axis=0), select_ref[...], preferred_element_type=jnp.float32)
        placed = placed.astype(bf16)
        for g in range(auxb // 4):
            parts = [placed[h * chunk:(h + 1) * chunk] for h in (2 * g, 2 * g + 1)]
            lanes = slice(g * 128, (g + 1) * 128)
            for q in range(4):
                piece = jnp.concatenate([part[:, q * 64:(q + 1) * 64] for part in parts], axis=1)
                if q == 0:
                    low_ref[0, rows, lanes] = jnp.where(first, piece, zero)
                    high_ref[3, rows, lanes] = jnp.where(first, zero, piece)
                    continue
                high_ref[q - 1, rows, lanes] = piece
                if q <= 2:
                    low_ref[q, rows, lanes] = piece
        part = pl.ds(begin, chunk)
        for m, (source, target) in enumerate(((low_ref, low_hbm), (high_ref, high_hbm))):
            copy = pltpu.make_async_copy(source.at[:, part], target.at[:, part], out_sem.at[n, m])
            copy.start()
            stores.append(copy)
    for copy in tiles:
        copy.wait()
    by_offset(row_ref, tiles_ref, even_ref, odd_ref)
    targets = [even_hbm] + [odd_hbm.at[to] for to in range(4)]
    for n, target in enumerate(targets):
        copy = pltpu.make_async_copy(odd_ref if n else even_ref, target, tile_sem.at[2 + n])
        copy.start()
        stores.append(copy)
    for copy in stores:
        copy.wait()


def align(slabs, start, count, row, density, direction):
    rows, auxb, _ = slabs.shape
    steps = len(CHUNKS)
    depth = auxb * 32
    high = (4, rows, depth)
    low = (3, rows, depth)
    tiles = (4,) + density.shape[2:]
    bf16 = jnp.bfloat16
    dma = pltpu.SemaphoreType.DMA
    return pl.pallas_call(
        functools.partial(align_kernel, CHUNKS),
        in_specs=[spec(pl.ANY)] * 6,
        out_specs=[spec(pl.ANY)] * 4,
        out_shape=[jax.ShapeDtypeStruct(shape, bf16) for shape in (high, low, tiles, (4,) + tiles)],
        scratch_shapes=[
            SMEM((1, 1), jnp.int32),
            SMEM((1, 1), jnp.int32),
            SMEM(row.shape, jnp.int32),
            VMEM(slabs.shape, bf16),
            VMEM((256, 256), bf16),
            VMEM(high, bf16),
            VMEM(low, bf16),
            VMEM((2,) + density.shape[1:], bf16),
            VMEM(tiles, bf16),
            VMEM(tiles, bf16),
            dma((3,)),
            dma((steps,)),
            dma((steps, 2)),
            dma((7,)),
        ],
        compiler_params=pltpu.CompilerParams(vmem_limit_bytes=60 * MIB),
    )(start[None], count[None], row, slabs, density, direction)


def product(left, right):
    total = None
    for a, b in zip(left, right):
        term = lax.dot_general(a, b, NT, preferred_element_type=jnp.float32)
        total = term if total is None else total + term
    return total


def tile_sums(tile, place, weights_ref):
    parts = []
    for which in range(2):
        total = jnp.zeros((8, 256), jnp.float32)
        for source in range(4):
            weight = weights_ref[source, place * 2 + which].astype(jnp.float32)
            piece = weight * tile[source * 64:(source + 1) * 64]
            total = total + jnp.sum(piece.reshape(8, 8, 256), axis=0)
        parts.append(total)
    return parts


def own_kernel(high_ref, low_ref, even_ref, tile_ref, out_ref):
    own = [low_ref[0]] + [high_ref[q] for q in range(4)]
    tile = product(own, own)
    tile_ref[...] = tile
    for to in range(4):
        out_ref[to, 0:4] = even_ref[...]
        out_ref[to, 4] = tile[to * 64:(to + 1) * 64].astype(jnp.bfloat16)


def near_kernel(high_ref, low_ref, before_ref, tile_ref, even_ref, out_ref, own_ref, sums_ref):
    own = [low_ref[0]] + [high_ref[q] for q in range(3)]
    out_ref[...] = product([before_ref[q] for q in range(4)], own)
    sums = tile_sums(tile_ref, 0, even_ref)
    for which in range(2):
        sums_ref[which] = sums[which]
    total = even_ref[0, 4].astype(jnp.float32)
    for source in range(1, 4):
        total = total + even_ref[source, 4].astype(jnp.float32)
    own_ref[...] = total.astype(jnp.bfloat16)


def far_kernel(high_ref, before_ref, after_ref, even_ref, odd_ref, near_ref, sums_in_ref, out_ref):
    t2 = product([high_ref[q + 1] for q in range(3)], [after_ref[q] for q in range(3)])
    t3 = product([before_ref[q + 2] for q in range(2)], [after_ref[q] for q in range(2)])
    sums = [sums_in_ref[0], sums_in_ref[1]]
    for tile, place, weights_ref in ((near_ref, 0, odd_ref), (t2, 1, even_ref), (t3, 1, odd_ref)):
        sums = [a + b for a, b in zip(sums, tile_sums(tile, place, weights_ref))]
    for to in range(4):
        part = slice(to * 64, (to + 1) * 64)
        for n, tile in enumerate((near_ref[part], t3[part], t2[part])):
            out_ref[to, n * 64:(n + 1) * 64] = tile.astype(jnp.bfloat16)
    lines = []
    for total in sums:
        value = jnp.broadcast_to(jnp.sum(total, keepdims=True), (8, 256))
        high = value.astype(jnp.bfloat16).astype(jnp.float32)
        rest = value - high
        middle = rest.astype(jnp.bfloat16).astype(jnp.float32)
        lines.append((high, middle, rest - middle))
    line = lax.broadcasted_iota(jnp.int32, (16, 256), 0)
    block = jnp.zeros((16, 256), jnp.float32)
    for which in range(2):
        for part in range(3):
            twice = jnp.concatenate([lines[which][part]] * 2, axis=0)
            block = jnp.where(line == which * 3 + part, twice, block)
    for to in range(4):
        out_ref[to, 192:208] = block.astype(jnp.bfloat16)


def sum_kernel(parts_ref, before_ref, own_ref, energy_ref):
    for n in range(3):
        rows = slice(n * 64, (n + 1) * 64)
        total = parts_ref[0, rows].astype(jnp.float32)
        for source in range(1, 4):
            total = total + parts_ref[source, rows].astype(jnp.float32)
        if n < 2:
            before_ref[n] = total.astype(jnp.bfloat16)
        else:
            own_ref[...] = total.astype(jnp.bfloat16)
    extra = parts_ref[0, 192:208].astype(jnp.float32)
    for source in range(1, 4):
        extra = extra + parts_ref[source, 192:208].astype(jnp.float32)
    first = extra[0:1] + extra[1:2] + extra[2:3]
    second = extra[3:4] + extra[4:5] + extra[5:6]
    lane = lax.broadcasted_iota(jnp.int32, (1, 128), 1)
    both = jnp.where(lane < 64, first[:, :128], second[:, :128])
    energy_ref[...] = jnp.broadcast_to(both[None], energy_ref.shape)


def finish_kernel(scale, row_ref, steps_ref, t0_ref, t2_ref, odd_ref, energy_ref, tiles_ref, out_ref):
    block = row_ref[0, 0]
    tiles = [t0_ref[...], odd_ref[0], t2_ref[...], odd_ref[1]]
    for s in range(4):
        other = row_ref[0, s]
        total = jnp.zeros(t0_ref.shape, jnp.float32)
        for k in range(4):
            chosen = (other >= 0) & (other - block == k)
            total = jnp.where(chosen, tiles[k].astype(jnp.float32), total)
        tiles_ref[0, s] = total.astype(jnp.bfloat16)
    total = jnp.sum(energy_ref[...], axis=0)
    first = total[0, 0]
    second = total[0, 64]
    for n in range(3):
        out_ref[n] = -0.5 * (first + steps_ref[n] * second) * scale


def kernel_call(kernel, in_specs, out_shape, limit=16, out_specs=None):
    return pl.pallas_call(
        kernel,
        in_specs=in_specs,
        out_specs=out_specs or [spec(VMEM)] * len(out_shape),
        out_shape=out_shape,
        compiler_params=pltpu.CompilerParams(vmem_limit_bytes=limit * MIB),
    )


def body(slabs, orbital_start, orbital_count, partners, density, direction, step_lengths):
    rows = slabs.shape[0]
    aux = lax.axis_size("aux")
    blocks = lax.axis_size("blk")
    slots = partners.shape[1]
    part = rows // aux

    def half(*shape):
        return jax.ShapeDtypeStruct(shape, jnp.bfloat16)

    def single(*shape):
        return jax.ShapeDtypeStruct(shape, jnp.float32)

    high, low, even, odd = align(slabs, orbital_start, orbital_count, partners, density, direction)
    after = moved_by(low, "blk", -2)
    before = moved_by(high, "blk", 1)
    odd = lax.all_to_all(odd, "aux", 0, 0, tiled=True)
    odd = moved_by(odd, "blk", 1)

    t0, even = kernel_call(own_kernel, [spec(VMEM)] * 3, [single(rows, rows), half(aux, 5, part, rows)])(
        high, low, even
    )
    even = lax.all_to_all(even, "aux", 0, 0, tiled=True)
    t1, t0, sums = kernel_call(
        near_kernel, [spec(VMEM)] * 5, [single(rows, rows), half(part, rows), single(2, 8, rows)]
    )(high, low, before, t0, even)
    (far,) = kernel_call(far_kernel, [spec(VMEM)] * 7, [half(aux, 3 * part + 16, rows)])(
        high, before, after, even, odd, t1, sums
    )
    far = lax.all_to_all(far, "aux", 0, 0, tiled=True)
    odd, t2, energy = kernel_call(
        sum_kernel, [spec(VMEM)], [half(2, part, rows), half(part, rows), single(blocks, 1, 128)]
    )(far)
    odd = moved_by(odd, "blk", -1)
    energy = lax.all_to_all(energy, "blk", 0, 0, tiled=True)

    scale = 1.0 / (rows * math.sqrt(blocks * slots))
    return kernel_call(
        functools.partial(finish_kernel, scale),
        [spec(SMEM)] * 2 + [spec(VMEM)] * 4,
        [half(1, slots, part, rows), single(3)],
        out_specs=[spec(VMEM), spec(SMEM)],
    )(partners, step_lengths, t0, t2, odd, energy)


def solution(mesh):
    return jax.shard_map(
        body,
        mesh=mesh,
        in_specs=(
            P("blk", "aux", None),
            P("blk"),
            P("blk"),
            P("blk", None),
            P("blk", None, "aux", None),
            P("blk", None, "aux", None),
            P(),
        ),
        out_specs=(P("blk", None, "aux", None), P()),
        check_vma=False,
    )
```

```python
import functools
import math

import jax
import jax.numpy as jnp
from jax import lax
from jax.experimental import pallas as pl
from jax.experimental.pallas import tpu as pltpu
from jax.sharding import PartitionSpec as P

VMEM = pltpu.VMEM
SMEM = pltpu.SMEM
NT = (((1,), (1,)), ((), ()))
MIB = 1024 * 1024
CHUNKS = (64, 128, 64)


def spec(space):
    return pl.BlockSpec(memory_space=space)


def moved_by(value, axis, steps):
    count = lax.axis_size(axis)
    pairs = [(source, source + steps) for source in range(count) if 0 <= source + steps < count]
    return lax.ppermute(value, axis, pairs)


def align_kernel(chunks, start_hbm, count_hbm, slab_ref, mid_ref, top_ref, low_ref, start_ref, count_ref, select_ref, sem):
    _, auxb, _ = slab_ref.shape
    bf16 = jnp.bfloat16
    small = [
        pltpu.make_async_copy(source, target, sem.at[n])
        for n, (source, target) in enumerate(((start_hbm, start_ref), (count_hbm, count_ref)))
    ]
    for copy in small:
        copy.start()
    for copy in small:
        copy.wait()
    shift = start_ref[0] & 31
    count = count_ref[0]
    a = lax.broadcasted_iota(jnp.int32, (128, 256), 0)
    to = lax.broadcasted_iota(jnp.int32, (128, 256), 1)
    hit = (a < count) & (((a + shift) & 127) == ((to >> 6) << 5) + (to & 31))
    for m in range(2):
        select_ref[m * 128:(m + 1) * 128] = jnp.where(hit & (((to >> 5) & 1) == m), 1.0, 0.0).astype(bf16)
    begin = 0
    for chunk in chunks:
        first = (lax.broadcasted_iota(jnp.int32, (chunk, 128), 1) & 31) >= shift
        zero = jnp.zeros((chunk, 128), bf16)
        rows = slice(begin, begin + chunk)
        begin += chunk
        by_function = jnp.swapaxes(slab_ref[rows], 0, 1)
        pairs = [jnp.concatenate([by_function[p], by_function[p + 1]], axis=1) for p in range(0, auxb, 2)]
        placed = jnp.dot(jnp.concatenate(pairs, axis=0), select_ref[...], preferred_element_type=jnp.float32)
        placed = placed.astype(bf16)
        for g in range(auxb // 4):
            parts = [placed[h * chunk:(h + 1) * chunk] for h in (2 * g, 2 * g + 1)]
            lanes = slice(g * 128, (g + 1) * 128)
            for q in range(4):
                piece = jnp.concatenate([part[:, q * 64:(q + 1) * 64] for part in parts], axis=1)
                if q == 0:
                    low_ref[0, rows, lanes] = jnp.where(first, piece, zero)
                    top_ref[1, rows, lanes] = jnp.where(first, zero, piece)
                    continue
                if q == 3:
                    top_ref[0, rows, lanes] = piece
                else:
                    mid_ref[q - 1, rows, lanes] = piece
                    low_ref[q, rows, lanes] = piece


def align(slabs, start, count):
    rows, auxb, _ = slabs.shape
    depth = auxb * 32
    bf16 = jnp.bfloat16
    return pl.pallas_call(
        functools.partial(align_kernel, CHUNKS),
        in_specs=[spec(pl.ANY)] * 2 + [spec(VMEM)],
        out_specs=[spec(VMEM)] * 3,
        out_shape=[jax.ShapeDtypeStruct((groups, rows, depth), bf16) for groups in (2, 2, 3)],
        scratch_shapes=[
            SMEM((1,), jnp.int32),
            SMEM((1,), jnp.int32),
            VMEM((256, 256), bf16),
            pltpu.SemaphoreType.DMA((2,)),
        ],
        compiler_params=pltpu.CompilerParams(vmem_limit_bytes=24 * MIB),
    )(start, count, slabs)


def by_offset_kernel(row_ref, density_ref, direction_ref, even_ref, odd_ref):
    block = row_ref[0, 0]
    for k in range(4):
        for which, source in enumerate((density_ref, direction_ref)):
            total = jnp.zeros(source.shape[2:], jnp.float32)
            for s in range(4):
                other = row_ref[0, s]
                full = 1.0 if s == 0 else 2.0
                weight = jnp.where((other >= 0) & (other - block == k), full, 0.0)
                total = total + weight * source[0, s].astype(jnp.float32)
            total = total.astype(jnp.bfloat16)
            place = k // 2 * 2 + which
            if k % 2 == 0:
                even_ref[place] = total
            else:
                for to in range(4):
                    odd_ref[to, place] = total


def product(left, right):
    total = None
    for a, b in zip(left, right):
        term = lax.dot_general(a, b, NT, preferred_element_type=jnp.float32)
        total = term if total is None else total + term
    return total


def tile_sums(tile, place, weights_ref):
    parts = []
    for which in range(2):
        total = jnp.zeros((8, 256), jnp.float32)
        for source in range(4):
            weight = weights_ref[source, place * 2 + which].astype(jnp.float32)
            piece = weight * tile[source * 64:(source + 1) * 64]
            total = total + jnp.sum(piece.reshape(8, 8, 256), axis=0)
        parts.append(total)
    return parts


def own_kernel(mid_ref, top_ref, low_ref, even_ref, tile_ref, out_ref):
    own = [low_ref[0], mid_ref[0], mid_ref[1], top_ref[0], top_ref[1]]
    tile = product(own, own)
    tile_ref[...] = tile
    for to in range(4):
        out_ref[to, 0:4] = even_ref[...]
        out_ref[to, 4] = tile[to * 64:(to + 1) * 64].astype(jnp.bfloat16)


def near_kernel(mid_ref, top_ref, low_ref, before_mid_ref, before_top_ref, tile_ref, even_ref, out_ref, own_ref, sums_ref):
    own = [low_ref[0], mid_ref[0], mid_ref[1], top_ref[0]]
    before = [before_mid_ref[0], before_mid_ref[1], before_top_ref[0], before_top_ref[1]]
    out_ref[...] = product(before, own)
    sums = tile_sums(tile_ref, 0, even_ref)
    for which in range(2):
        sums_ref[which] = sums[which]
    total = even_ref[0, 4].astype(jnp.float32)
    for source in range(1, 4):
        total = total + even_ref[source, 4].astype(jnp.float32)
    own_ref[...] = total.astype(jnp.bfloat16)


def far_kernel(mid_ref, top_ref, before_ref, after_ref, even_ref, odd_ref, near_ref, sums_in_ref, out_ref):
    after = [after_ref[q] for q in range(3)]
    t2 = product([mid_ref[1], top_ref[0], top_ref[1]], after)
    t3 = product([before_ref[q] for q in range(2)], after)
    sums = [sums_in_ref[0], sums_in_ref[1]]
    for tile, place, weights_ref in ((near_ref, 0, odd_ref), (t2, 1, even_ref), (t3, 1, odd_ref)):
        sums = [a + b for a, b in zip(sums, tile_sums(tile, place, weights_ref))]
    for to in range(4):
        part = slice(to * 64, (to + 1) * 64)
        for n, tile in enumerate((near_ref[part], t3[part], t2[part])):
            out_ref[to, n * 64:(n + 1) * 64] = tile.astype(jnp.bfloat16)
    lines = []
    for total in sums:
        value = jnp.broadcast_to(jnp.sum(total, keepdims=True), (8, 256))
        high = value.astype(jnp.bfloat16).astype(jnp.float32)
        rest = value - high
        middle = rest.astype(jnp.bfloat16).astype(jnp.float32)
        lines.append((high, middle, rest - middle))
    line = lax.broadcasted_iota(jnp.int32, (16, 256), 0)
    block = jnp.zeros((16, 256), jnp.float32)
    for which in range(2):
        for part in range(3):
            twice = jnp.concatenate([lines[which][part]] * 2, axis=0)
            block = jnp.where(line == which * 3 + part, twice, block)
    for to in range(4):
        out_ref[to, 192:208] = block.astype(jnp.bfloat16)


def sum_kernel(parts_ref, before_ref, own_ref, energy_ref):
    for n in range(3):
        rows = slice(n * 64, (n + 1) * 64)
        total = parts_ref[0, rows].astype(jnp.float32)
        for source in range(1, 4):
            total = total + parts_ref[source, rows].astype(jnp.float32)
        if n < 2:
            before_ref[n] = total.astype(jnp.bfloat16)
        else:
            own_ref[...] = total.astype(jnp.bfloat16)
    extra = parts_ref[0, 192:208].astype(jnp.float32)
    for source in range(1, 4):
        extra = extra + parts_ref[source, 192:208].astype(jnp.float32)
    first = extra[0:1] + extra[1:2] + extra[2:3]
    second = extra[3:4] + extra[4:5] + extra[5:6]
    lane = lax.broadcasted_iota(jnp.int32, (1, 128), 1)
    both = jnp.where(lane < 64, first[:, :128], second[:, :128])
    energy_ref[...] = jnp.broadcast_to(both[None], energy_ref.shape)


def finish_kernel(scale, row_ref, steps_ref, t0_ref, t2_ref, odd_ref, energy_ref, tiles_ref, out_ref):
    block = row_ref[0, 0]
    tiles = [t0_ref[...], odd_ref[0], t2_ref[...], odd_ref[1]]
    for s in range(4):
        other = row_ref[0, s]
        total = jnp.zeros(t0_ref.shape, jnp.float32)
        for k in range(4):
            chosen = (other >= 0) & (other - block == k)
            total = jnp.where(chosen, tiles[k].astype(jnp.float32), total)
        tiles_ref[0, s] = total.astype(jnp.bfloat16)
    total = jnp.sum(energy_ref[...], axis=0)
    first = total[0, 0]
    second = total[0, 64]
    for n in range(3):
        out_ref[n] = -0.5 * (first + steps_ref[n] * second) * scale


def kernel_call(kernel, in_specs, out_shape, limit=16, out_specs=None):
    return pl.pallas_call(
        kernel,
        in_specs=in_specs,
        out_specs=out_specs or [spec(VMEM)] * len(out_shape),
        out_shape=out_shape,
        compiler_params=pltpu.CompilerParams(vmem_limit_bytes=limit * MIB),
    )


def body(slabs, orbital_start, orbital_count, partners, density, direction, step_lengths):
    rows = slabs.shape[0]
    aux = lax.axis_size("aux")
    blocks = lax.axis_size("blk")
    slots = partners.shape[1]
    part = rows // aux

    def half(*shape):
        return jax.ShapeDtypeStruct(shape, jnp.bfloat16)

    def single(*shape):
        return jax.ShapeDtypeStruct(shape, jnp.float32)

    mid, top, low = align(slabs, orbital_start, orbital_count)
    after = moved_by(low, "blk", -2)
    before_mid = moved_by(mid, "blk", 1)
    before_top = moved_by(top, "blk", 1)
    low, density, direction = lax.optimization_barrier((low, density, direction))
    even, odd = kernel_call(by_offset_kernel, [spec(SMEM)] + [spec(VMEM)] * 2, [half(4, part, rows), half(aux, 4, part, rows)])(
        partners, density, direction
    )
    odd = lax.all_to_all(odd, "aux", 0, 0, tiled=True)
    odd = moved_by(odd, "blk", 1)

    t0, even = kernel_call(own_kernel, [spec(VMEM)] * 4, [single(rows, rows), half(aux, 5, part, rows)])(
        mid, top, low, even
    )
    even = lax.all_to_all(even, "aux", 0, 0, tiled=True)
    t1, t0, sums = kernel_call(
        near_kernel, [spec(VMEM)] * 7, [single(rows, rows), half(part, rows), single(2, 8, rows)]
    )(mid, top, low, before_mid, before_top, t0, even)
    (far,) = kernel_call(far_kernel, [spec(VMEM)] * 8, [half(aux, 3 * part + 16, rows)])(
        mid, top, before_top, after, even, odd, t1, sums
    )
    far = lax.all_to_all(far, "aux", 0, 0, tiled=True)
    odd, t2, energy = kernel_call(
        sum_kernel, [spec(VMEM)], [half(2, part, rows), half(part, rows), single(blocks, 1, 128)]
    )(far)
    odd = moved_by(odd, "blk", -1)
    energy = lax.all_to_all(energy, "blk", 0, 0, tiled=True)

    scale = 1.0 / (rows * math.sqrt(blocks * slots))
    return kernel_call(
        functools.partial(finish_kernel, scale),
        [spec(SMEM)] * 2 + [spec(VMEM)] * 4,
        [half(1, slots, part, rows), single(3)],
        out_specs=[spec(VMEM), spec(SMEM)],
    )(partners, step_lengths, t0, t2, odd, energy)


def solution(mesh):
    return jax.shard_map(
        body,
        mesh=mesh,
        in_specs=(
            P("blk", "aux", None),
            P("blk"),
            P("blk"),
            P("blk", None),
            P("blk", None, "aux", None),
            P("blk", None, "aux", None),
            P(),
        ),
        out_specs=(P("blk", None, "aux", None), P()),
        check_vma=False,
    )
```

```python
import functools
import math

import jax
import jax.numpy as jnp
from jax import lax
from jax.experimental import pallas as pl
from jax.experimental.pallas import tpu as pltpu
from jax.sharding import PartitionSpec as P

VMEM = pltpu.VMEM
SMEM = pltpu.SMEM
NT = (((1,), (1,)), ((), ()))
MIB = 1024 * 1024
CHUNKS = (64, 96, 96)


def spec(space):
    return pl.BlockSpec(memory_space=space)


def moved_by(value, axis, steps):
    count = lax.axis_size(axis)
    pairs = [(source, source + steps) for source in range(count) if 0 <= source + steps < count]
    return lax.ppermute(value, axis, pairs)


def align_kernel(
    chunks, start_ref, count_ref, slab_hbm, mid_ref, top_ref, low_ref, slab_ref, select_ref, sem
):
    _, auxb, _ = slab_ref.shape
    bf16 = jnp.bfloat16
    begins = [sum(chunks[:n]) for n in range(len(chunks))]
    loads = [
        pltpu.make_async_copy(slab_hbm.at[pl.ds(begin, chunk)], slab_ref.at[pl.ds(begin, chunk)], sem.at[n])
        for n, (begin, chunk) in enumerate(zip(begins, chunks))
    ]
    for copy in loads:
        copy.start()
    shift = start_ref[0] & 31
    count = count_ref[0]
    a = lax.broadcasted_iota(jnp.int32, (128, 256), 0)
    to = lax.broadcasted_iota(jnp.int32, (128, 256), 1)
    hit = (a < count) & (((a + shift) & 127) == ((to >> 6) << 5) + (to & 31))
    for m in range(2):
        select_ref[m * 128:(m + 1) * 128] = jnp.where(hit & (((to >> 5) & 1) == m), 1.0, 0.0).astype(bf16)
    for load, begin, chunk in zip(loads, begins, chunks):
        first = (lax.broadcasted_iota(jnp.int32, (chunk, 128), 1) & 31) >= shift
        zero = jnp.zeros((chunk, 128), bf16)
        rows = slice(begin, begin + chunk)
        load.wait()
        by_function = jnp.swapaxes(slab_ref[rows], 0, 1)
        pairs = [jnp.concatenate([by_function[p], by_function[p + 1]], axis=1) for p in range(0, auxb, 2)]
        placed = jnp.dot(jnp.concatenate(pairs, axis=0), select_ref[...], preferred_element_type=jnp.float32)
        placed = placed.astype(bf16)
        for g in range(auxb // 4):
            parts = [placed[h * chunk:(h + 1) * chunk] for h in (2 * g, 2 * g + 1)]
            lanes = slice(g * 128, (g + 1) * 128)
            for q in range(4):
                piece = jnp.concatenate([part[:, q * 64:(q + 1) * 64] for part in parts], axis=1)
                if q == 0:
                    low_ref[0, rows, lanes] = jnp.where(first, piece, zero)
                    top_ref[1, rows, lanes] = jnp.where(first, zero, piece)
                    continue
                if q == 3:
                    top_ref[0, rows, lanes] = piece
                else:
                    mid_ref[q - 1, rows, lanes] = piece
                    low_ref[q, rows, lanes] = piece


def align(slabs, start, count):
    rows, auxb, _ = slabs.shape
    depth = auxb * 32
    bf16 = jnp.bfloat16
    return pl.pallas_call(
        functools.partial(align_kernel, CHUNKS),
        in_specs=[spec(SMEM)] * 2 + [spec(pl.ANY)],
        out_specs=[spec(VMEM)] * 3,
        out_shape=[jax.ShapeDtypeStruct((groups, rows, depth), bf16) for groups in (2, 2, 3)],
        scratch_shapes=[
            VMEM(slabs.shape, bf16),
            VMEM((256, 256), bf16),
            pltpu.SemaphoreType.DMA((len(CHUNKS),)),
        ],
        compiler_params=pltpu.CompilerParams(vmem_limit_bytes=49 * MIB),
    )(start, count, slabs)


def by_offset_kernel(row_ref, density_ref, direction_ref, even_ref, odd_ref):
    block = row_ref[0, 0]
    for k in range(4):
        for which, source in enumerate((density_ref, direction_ref)):
            total = jnp.zeros(source.shape[2:], jnp.float32)
            for s in range(4):
                other = row_ref[0, s]
                full = 1.0 if s == 0 else 2.0
                weight = jnp.where((other >= 0) & (other - block == k), full, 0.0)
                total = total + weight * source[0, s].astype(jnp.float32)
            total = total.astype(jnp.bfloat16)
            place = k // 2 * 2 + which
            if k % 2 == 0:
                even_ref[place] = total
            else:
                for to in range(4):
                    odd_ref[to, place] = total


def product(left, right):
    total = None
    for a, b in zip(left, right):
        term = lax.dot_general(a, b, NT, preferred_element_type=jnp.float32)
        total = term if total is None else total + term
    return total


def tile_sums(tile, place, weights_ref):
    parts = []
    for which in range(2):
        total = jnp.zeros((8, 256), jnp.float32)
        for source in range(4):
            weight = weights_ref[source, place * 2 + which].astype(jnp.float32)
            piece = weight * tile[source * 64:(source + 1) * 64]
            total = total + jnp.sum(piece.reshape(8, 8, 256), axis=0)
        parts.append(total)
    return parts


def own_kernel(mid_ref, top_ref, low_ref, even_ref, tile_ref, out_ref):
    own = [low_ref[0], mid_ref[0], mid_ref[1], top_ref[0], top_ref[1]]
    tile = product(own, own)
    tile_ref[...] = tile
    for to in range(4):
        out_ref[to, 0:4] = even_ref[...]
        out_ref[to, 4] = tile[to * 64:(to + 1) * 64].astype(jnp.bfloat16)


def near_kernel(mid_ref, top_ref, low_ref, before_mid_ref, before_top_ref, tile_ref, even_ref, out_ref, own_ref, sums_ref):
    own = [low_ref[0], mid_ref[0], mid_ref[1], top_ref[0]]
    before = [before_mid_ref[0], before_mid_ref[1], before_top_ref[0], before_top_ref[1]]
    out_ref[...] = product(before, own)
    sums = tile_sums(tile_ref, 0, even_ref)
    for which in range(2):
        sums_ref[which] = sums[which]
    total = even_ref[0, 4].astype(jnp.float32)
    for source in range(1, 4):
        total = total + even_ref[source, 4].astype(jnp.float32)
    own_ref[...] = total.astype(jnp.bfloat16)


def far_kernel(mid_ref, top_ref, before_ref, after_ref, even_ref, odd_ref, near_ref, sums_in_ref, out_ref):
    after = [after_ref[q] for q in range(3)]
    t2 = product([mid_ref[1], top_ref[0], top_ref[1]], after)
    t3 = product([before_ref[q] for q in range(2)], after)
    sums = [sums_in_ref[0], sums_in_ref[1]]
    for tile, place, weights_ref in ((near_ref, 0, odd_ref), (t2, 1, even_ref), (t3, 1, odd_ref)):
        sums = [a + b for a, b in zip(sums, tile_sums(tile, place, weights_ref))]
    for to in range(4):
        part = slice(to * 64, (to + 1) * 64)
        for n, tile in enumerate((near_ref[part], t3[part], t2[part])):
            out_ref[to, n * 64:(n + 1) * 64] = tile.astype(jnp.bfloat16)
    lines = []
    for total in sums:
        value = jnp.broadcast_to(jnp.sum(total, keepdims=True), (8, 256))
        high = value.astype(jnp.bfloat16).astype(jnp.float32)
        rest = value - high
        middle = rest.astype(jnp.bfloat16).astype(jnp.float32)
        lines.append((high, middle, rest - middle))
    line = lax.broadcasted_iota(jnp.int32, (16, 256), 0)
    block = jnp.zeros((16, 256), jnp.float32)
    for which in range(2):
        for part in range(3):
            twice = jnp.concatenate([lines[which][part]] * 2, axis=0)
            block = jnp.where(line == which * 3 + part, twice, block)
    for to in range(4):
        out_ref[to, 192:208] = block.astype(jnp.bfloat16)


def sum_kernel(parts_ref, before_ref, own_ref, energy_ref):
    for n in range(3):
        rows = slice(n * 64, (n + 1) * 64)
        total = parts_ref[0, rows].astype(jnp.float32)
        for source in range(1, 4):
            total = total + parts_ref[source, rows].astype(jnp.float32)
        if n < 2:
            before_ref[n] = total.astype(jnp.bfloat16)
        else:
            own_ref[...] = total.astype(jnp.bfloat16)
    extra = parts_ref[0, 192:208].astype(jnp.float32)
    for source in range(1, 4):
        extra = extra + parts_ref[source, 192:208].astype(jnp.float32)
    first = extra[0:1] + extra[1:2] + extra[2:3]
    second = extra[3:4] + extra[4:5] + extra[5:6]
    lane = lax.broadcasted_iota(jnp.int32, (1, 128), 1)
    both = jnp.where(lane < 64, first[:, :128], second[:, :128])
    energy_ref[...] = jnp.broadcast_to(both[None], energy_ref.shape)


def finish_kernel(scale, row_ref, steps_ref, t0_ref, t2_ref, odd_ref, energy_ref, tiles_ref, out_ref):
    block = row_ref[0, 0]
    tiles = [t0_ref[...], odd_ref[0], t2_ref[...], odd_ref[1]]
    for s in range(4):
        other = row_ref[0, s]
        total = jnp.zeros(t0_ref.shape, jnp.float32)
        for k in range(4):
            chosen = (other >= 0) & (other - block == k)
            total = jnp.where(chosen, tiles[k].astype(jnp.float32), total)
        tiles_ref[0, s] = total.astype(jnp.bfloat16)
    total = jnp.sum(energy_ref[...], axis=0)
    first, second = total[:, :3], total[:, 64:67]
    out_ref[...] = -0.5 * (first + steps_ref[...] * second) * scale


def kernel_call(kernel, in_specs, out_shape, limit=16, out_specs=None):
    return pl.pallas_call(
        kernel,
        in_specs=in_specs,
        out_specs=out_specs or [spec(VMEM)] * len(out_shape),
        out_shape=out_shape,
        compiler_params=pltpu.CompilerParams(vmem_limit_bytes=limit * MIB),
    )


def body(slabs, orbital_start, orbital_count, partners, density, direction, step_lengths):
    rows = slabs.shape[0]
    aux = lax.axis_size("aux")
    blocks = lax.axis_size("blk")
    slots = partners.shape[1]
    part = rows // aux

    def half(*shape):
        return jax.ShapeDtypeStruct(shape, jnp.bfloat16)

    def single(*shape):
        return jax.ShapeDtypeStruct(shape, jnp.float32)

    mid, top, low = align(slabs, orbital_start, orbital_count)
    after = moved_by(low, "blk", -2)
    before_mid = moved_by(mid, "blk", 1)
    before_top = moved_by(top, "blk", 1)
    low, density, direction = lax.optimization_barrier((low, density, direction))
    even, odd = kernel_call(by_offset_kernel, [spec(SMEM)] + [spec(VMEM)] * 2, [half(4, part, rows), half(aux, 4, part, rows)])(
        partners, density, direction
    )
    odd = lax.all_to_all(odd, "aux", 0, 0, tiled=True)
    odd = moved_by(odd, "blk", 1)

    t0, even = kernel_call(own_kernel, [spec(VMEM)] * 4, [single(rows, rows), half(aux, 5, part, rows)])(
        mid, top, low, even
    )
    even = lax.all_to_all(even, "aux", 0, 0, tiled=True)
    t1, t0, sums = kernel_call(
        near_kernel, [spec(VMEM)] * 7, [single(rows, rows), half(part, rows), single(2, 8, rows)]
    )(mid, top, low, before_mid, before_top, t0, even)
    (far,) = kernel_call(far_kernel, [spec(VMEM)] * 8, [half(aux, 3 * part + 16, rows)])(
        mid, top, before_top, after, even, odd, t1, sums
    )
    far = lax.all_to_all(far, "aux", 0, 0, tiled=True)
    odd, t2, energy = kernel_call(
        sum_kernel, [spec(VMEM)], [half(2, part, rows), half(part, rows), single(blocks, 1, 128)]
    )(far)
    odd = moved_by(odd, "blk", -1)
    energy = lax.all_to_all(energy, "blk", 0, 0, tiled=True)

    scale = 1.0 / (rows * math.sqrt(blocks * slots))
    tiles, energies = kernel_call(
        functools.partial(finish_kernel, scale),
        [spec(SMEM)] + [spec(VMEM)] * 5,
        [half(1, slots, part, rows), single(1, 3)],
    )(partners, step_lengths[None], t0, t2, odd, energy)
    return tiles, energies[0]


def solution(mesh):
    return jax.shard_map(
        body,
        mesh=mesh,
        in_specs=(
            P("blk", "aux", None),
            P("blk"),
            P("blk"),
            P("blk", None),
            P("blk", None, "aux", None),
            P("blk", None, "aux", None),
            P(),
        ),
        out_specs=(P("blk", None, "aux", None), P()),
        check_vma=False,
    )
```

```python
import functools
import math

import jax
import jax.numpy as jnp
from jax import lax
from jax.experimental import pallas as pl
from jax.experimental.pallas import tpu as pltpu
from jax.sharding import PartitionSpec as P

VMEM = pltpu.VMEM
SMEM = pltpu.SMEM
NT = (((1,), (1,)), ((), ()))
MIB = 1024 * 1024
CHUNKS = (64, 96, 96)


def spec(space):
    return pl.BlockSpec(memory_space=space)


def moved_by(value, axis, steps):
    count = lax.axis_size(axis)
    pairs = [(source, source + steps) for source in range(count) if 0 <= source + steps < count]
    return lax.ppermute(value, axis, pairs)


def align_kernel(
    chunks, start_ref, count_ref, slab_hbm, mid_ref, top_ref, low_ref, slab_ref, select_ref, sem
):
    _, auxb, _ = slab_ref.shape
    bf16 = jnp.bfloat16
    begins = [sum(chunks[:n]) for n in range(len(chunks))]
    loads = [
        pltpu.make_async_copy(slab_hbm.at[pl.ds(begin, chunk)], slab_ref.at[pl.ds(begin, chunk)], sem.at[n])
        for n, (begin, chunk) in enumerate(zip(begins, chunks))
    ]
    for copy in loads:
        copy.start()
    shift = start_ref[0] & 31
    count = count_ref[0]
    a = lax.broadcasted_iota(jnp.int32, (128, 256), 0)
    to = lax.broadcasted_iota(jnp.int32, (128, 256), 1)
    hit = (a < count) & (((a + shift) & 127) == ((to >> 6) << 5) + (to & 31))
    for m in range(2):
        select_ref[m * 128:(m + 1) * 128] = jnp.where(hit & (((to >> 5) & 1) == m), 1.0, 0.0).astype(bf16)
    for load, begin, chunk in zip(loads, begins, chunks):
        first = (lax.broadcasted_iota(jnp.int32, (chunk, 128), 1) & 31) >= shift
        zero = jnp.zeros((chunk, 128), bf16)
        rows = slice(begin, begin + chunk)
        load.wait()
        by_function = jnp.swapaxes(slab_ref[rows], 0, 1)
        pairs = [jnp.concatenate([by_function[p], by_function[p + 1]], axis=1) for p in range(0, auxb, 2)]
        placed = jnp.dot(jnp.concatenate(pairs, axis=0), select_ref[...], preferred_element_type=jnp.float32)
        placed = placed.astype(bf16)
        for g in range(auxb // 4):
            parts = [placed[h * chunk:(h + 1) * chunk] for h in (2 * g, 2 * g + 1)]
            lanes = slice(g * 128, (g + 1) * 128)
            for q in range(4):
                piece = jnp.concatenate([part[:, q * 64:(q + 1) * 64] for part in parts], axis=1)
                if q == 0:
                    low_ref[0, rows, lanes] = jnp.where(first, piece, zero)
                    top_ref[1, rows, lanes] = jnp.where(first, zero, piece)
                    continue
                if q == 3:
                    top_ref[0, rows, lanes] = piece
                else:
                    mid_ref[q - 1, rows, lanes] = piece
                    low_ref[q, rows, lanes] = piece


def align(slabs, start, count):
    rows, auxb, _ = slabs.shape
    depth = auxb * 32
    bf16 = jnp.bfloat16
    return pl.pallas_call(
        functools.partial(align_kernel, CHUNKS),
        in_specs=[spec(SMEM)] * 2 + [spec(pl.ANY)],
        out_specs=[spec(VMEM)] * 3,
        out_shape=[jax.ShapeDtypeStruct((groups, rows, depth), bf16) for groups in (2, 2, 3)],
        scratch_shapes=[
            VMEM(slabs.shape, bf16),
            VMEM((256, 256), bf16),
            pltpu.SemaphoreType.DMA((len(CHUNKS),)),
        ],
        compiler_params=pltpu.CompilerParams(vmem_limit_bytes=49 * MIB),
    )(start, count, slabs)


def by_offset_kernel(row_ref, density_ref, direction_ref, even_ref, odd_ref):
    block = row_ref[0, 0]
    for k in range(4):
        for which, source in enumerate((density_ref, direction_ref)):
            total = jnp.zeros(source.shape[2:], jnp.float32)
            for s in range(4):
                other = row_ref[0, s]
                full = 1.0 if s == 0 else 2.0
                weight = jnp.where((other >= 0) & (other - block == k), full, 0.0)
                total = total + weight * source[0, s].astype(jnp.float32)
            total = total.astype(jnp.bfloat16)
            if k % 2 == 0:
                even_ref[k // 2 * 2 + which] = total
            else:
                for to in range(4):
                    odd_ref[to, k // 2 * 2 + which] = total


def product(left, right):
    total = None
    for a, b in zip(left, right):
        term = lax.dot_general(a, b, NT, preferred_element_type=jnp.float32)
        total = term if total is None else total + term
    return total


def tile_sums(tile, place, weights_ref):
    parts = []
    for which in range(2):
        total = jnp.zeros((8, 256), jnp.float32)
        for source in range(4):
            weight = weights_ref[source, place * 2 + which].astype(jnp.float32)
            piece = weight * tile[source * 64:(source + 1) * 64]
            total = total + jnp.sum(piece.reshape(8, 8, 256), axis=0)
        parts.append(total)
    return parts


def own_kernel(mid_ref, top_ref, low_ref, even_ref, out_ref):
    own = [low_ref[0], mid_ref[0], mid_ref[1], top_ref[0], top_ref[1]]
    tile = product(own, own)
    high = tile.astype(jnp.bfloat16)
    rest = (tile - high.astype(jnp.float32)).astype(jnp.bfloat16)
    for to in range(4):
        part = slice(to * 64, (to + 1) * 64)
        out_ref[to, 0] = even_ref[2]
        out_ref[to, 1] = even_ref[3]
        out_ref[to, 2] = high[part]
        out_ref[to, 3] = rest[part]


def near_kernel(mid_ref, top_ref, low_ref, before_mid_ref, before_top_ref, even_ref, local_ref, out_ref, own_ref, sums_ref):
    own = [low_ref[0], mid_ref[0], mid_ref[1], top_ref[0]]
    before = [before_mid_ref[0], before_mid_ref[1], before_top_ref[0], before_top_ref[1]]
    out_ref[...] = product(before, own)
    total = even_ref[0, 2].astype(jnp.float32) + even_ref[0, 3].astype(jnp.float32)
    for source in range(1, 4):
        total = total + even_ref[source, 2].astype(jnp.float32) + even_ref[source, 3].astype(jnp.float32)
    own_ref[...] = total.astype(jnp.bfloat16)
    for which in range(2):
        sums_ref[which] = jnp.sum((local_ref[which].astype(jnp.float32) * total).reshape(8, 8, 256), axis=0)


def far_kernel(mid_ref, top_ref, before_ref, after_ref, even_ref, odd_ref, near_ref, sums_in_ref, out_ref):
    after = [after_ref[q] for q in range(3)]
    t2 = product([mid_ref[1], top_ref[0], top_ref[1]], after)
    t3 = product([before_ref[q] for q in range(2)], after)
    sums = [sums_in_ref[0], sums_in_ref[1]]
    for tile, place, weights_ref in ((near_ref, 0, odd_ref), (t2, 0, even_ref), (t3, 1, odd_ref)):
        sums = [a + b for a, b in zip(sums, tile_sums(tile, place, weights_ref))]
    for to in range(4):
        part = slice(to * 64, (to + 1) * 64)
        for n, tile in enumerate((near_ref[part], t3[part], t2[part])):
            out_ref[to, n * 64:(n + 1) * 64] = tile.astype(jnp.bfloat16)
    lines = []
    for total in sums:
        value = jnp.broadcast_to(jnp.sum(total, keepdims=True), (8, 256))
        high = value.astype(jnp.bfloat16).astype(jnp.float32)
        rest = value - high
        middle = rest.astype(jnp.bfloat16).astype(jnp.float32)
        lines.append((high, middle, rest - middle))
    line = lax.broadcasted_iota(jnp.int32, (16, 256), 0)
    block = jnp.zeros((16, 256), jnp.float32)
    for which in range(2):
        for part in range(3):
            twice = jnp.concatenate([lines[which][part]] * 2, axis=0)
            block = jnp.where(line == which * 3 + part, twice, block)
    for to in range(4):
        out_ref[to, 192:208] = block.astype(jnp.bfloat16)


def sum_kernel(parts_ref, before_ref, own_ref, energy_ref):
    for n in range(3):
        rows = slice(n * 64, (n + 1) * 64)
        total = parts_ref[0, rows].astype(jnp.float32)
        for source in range(1, 4):
            total = total + parts_ref[source, rows].astype(jnp.float32)
        if n < 2:
            before_ref[n] = total.astype(jnp.bfloat16)
        else:
            own_ref[...] = total.astype(jnp.bfloat16)
    extra = parts_ref[0, 192:208].astype(jnp.float32)
    for source in range(1, 4):
        extra = extra + parts_ref[source, 192:208].astype(jnp.float32)
    first = extra[0:1] + extra[1:2] + extra[2:3]
    second = extra[3:4] + extra[4:5] + extra[5:6]
    lane = lax.broadcasted_iota(jnp.int32, (1, 128), 1)
    both = jnp.where(lane < 64, first[:, :128], second[:, :128])
    energy_ref[...] = jnp.broadcast_to(both[None], energy_ref.shape)


def finish_kernel(scale, row_ref, steps_ref, t0_ref, t2_ref, odd_ref, energy_ref, tiles_ref, out_ref):
    block = row_ref[0, 0]
    tiles = [t0_ref[...], odd_ref[0], t2_ref[...], odd_ref[1]]
    for s in range(4):
        other = row_ref[0, s]
        total = jnp.zeros(t0_ref.shape, jnp.float32)
        for k in range(4):
            chosen = (other >= 0) & (other - block == k)
            total = jnp.where(chosen, tiles[k].astype(jnp.float32), total)
        tiles_ref[0, s] = total.astype(jnp.bfloat16)
    total = jnp.sum(energy_ref[...], axis=0)
    first, second = total[:, :3], total[:, 64:67]
    out_ref[...] = -0.5 * (first + steps_ref[...] * second) * scale


def kernel_call(kernel, in_specs, out_shape, limit=16, out_specs=None):
    return pl.pallas_call(
        kernel,
        in_specs=in_specs,
        out_specs=out_specs or [spec(VMEM)] * len(out_shape),
        out_shape=out_shape,
        compiler_params=pltpu.CompilerParams(vmem_limit_bytes=limit * MIB),
    )


def body(slabs, orbital_start, orbital_count, partners, density, direction, step_lengths):
    rows = slabs.shape[0]
    aux = lax.axis_size("aux")
    blocks = lax.axis_size("blk")
    slots = partners.shape[1]
    part = rows // aux

    def half(*shape):
        return jax.ShapeDtypeStruct(shape, jnp.bfloat16)

    def single(*shape):
        return jax.ShapeDtypeStruct(shape, jnp.float32)

    mid, top, low = align(slabs, orbital_start, orbital_count)
    after = moved_by(low, "blk", -2)
    before_mid = moved_by(mid, "blk", 1)
    before_top = moved_by(top, "blk", 1)
    low, density, direction = lax.optimization_barrier((low, density, direction))
    even, odd = kernel_call(by_offset_kernel, [spec(SMEM)] + [spec(VMEM)] * 2, [half(4, part, rows), half(aux, 4, part, rows)])(
        partners, density, direction
    )
    odd = lax.all_to_all(odd, "aux", 0, 0, tiled=True)
    odd = moved_by(odd, "blk", 1)

    local = even
    (even,) = kernel_call(own_kernel, [spec(VMEM)] * 4, [half(aux, 4, part, rows)])(mid, top, low, local)
    even = lax.all_to_all(even, "aux", 0, 0, tiled=True)
    t1, t0, sums = kernel_call(
        near_kernel, [spec(VMEM)] * 7, [single(rows, rows), half(part, rows), single(2, 8, rows)]
    )(mid, top, low, before_mid, before_top, even, local)
    (far,) = kernel_call(far_kernel, [spec(VMEM)] * 8, [half(aux, 3 * part + 16, rows)])(
        mid, top, before_top, after, even, odd, t1, sums
    )
    far = lax.all_to_all(far, "aux", 0, 0, tiled=True)
    odd, t2, energy = kernel_call(
        sum_kernel, [spec(VMEM)], [half(2, part, rows), half(part, rows), single(blocks, 1, 128)]
    )(far)
    odd = moved_by(odd, "blk", -1)
    energy = lax.all_to_all(energy, "blk", 0, 0, tiled=True)

    scale = 1.0 / (rows * math.sqrt(blocks * slots))
    tiles, energies = kernel_call(
        functools.partial(finish_kernel, scale),
        [spec(SMEM)] + [spec(VMEM)] * 5,
        [half(1, slots, part, rows), single(1, 3)],
    )(partners, step_lengths[None], t0, t2, odd, energy)
    return tiles, energies[0]


def solution(mesh):
    return jax.shard_map(
        body,
        mesh=mesh,
        in_specs=(
            P("blk", "aux", None),
            P("blk"),
            P("blk"),
            P("blk", None),
            P("blk", None, "aux", None),
            P("blk", None, "aux", None),
            P(),
        ),
        out_specs=(P("blk", None, "aux", None), P()),
        check_vma=False,
    )
```

```python
import functools
import math

import jax
import jax.numpy as jnp
from jax import lax
from jax.experimental import pallas as pl
from jax.experimental.pallas import tpu as pltpu
from jax.sharding import PartitionSpec as P

VMEM = pltpu.VMEM
SMEM = pltpu.SMEM
NT = (((1,), (1,)), ((), ()))
MIB = 1024 * 1024
CHUNKS = (64, 96, 96)


def spec(space):
    return pl.BlockSpec(memory_space=space)


def moved_by(value, axis, steps):
    count = lax.axis_size(axis)
    pairs = [(source, source + steps) for source in range(count) if 0 <= source + steps < count]
    return lax.ppermute(value, axis, pairs)


def align_kernel(
    chunks, start_ref, count_ref, slab_hbm, mid_ref, top_ref, low_ref, slab_ref, select_ref, sem
):
    _, auxb, _ = slab_ref.shape
    bf16 = jnp.bfloat16
    begins = [sum(chunks[:n]) for n in range(len(chunks))]
    loads = [
        pltpu.make_async_copy(slab_hbm.at[pl.ds(begin, chunk)], slab_ref.at[pl.ds(begin, chunk)], sem.at[n])
        for n, (begin, chunk) in enumerate(zip(begins, chunks))
    ]
    for copy in loads:
        copy.start()
    shift = start_ref[0] & 31
    count = count_ref[0]
    a = lax.broadcasted_iota(jnp.int32, (128, 256), 0)
    to = lax.broadcasted_iota(jnp.int32, (128, 256), 1)
    hit = (a < count) & (((a + shift) & 127) == ((to >> 6) << 5) + (to & 31))
    for m in range(2):
        select_ref[m * 128:(m + 1) * 128] = jnp.where(hit & (((to >> 5) & 1) == m), 1.0, 0.0).astype(bf16)
    for load, begin, chunk in zip(loads, begins, chunks):
        first = (lax.broadcasted_iota(jnp.int32, (chunk, 128), 1) & 31) >= shift
        zero = jnp.zeros((chunk, 128), bf16)
        rows = slice(begin, begin + chunk)
        load.wait()
        by_function = jnp.swapaxes(slab_ref[rows], 0, 1)
        pairs = [jnp.concatenate([by_function[p], by_function[p + 1]], axis=1) for p in range(0, auxb, 2)]
        placed = jnp.dot(jnp.concatenate(pairs, axis=0), select_ref[...], preferred_element_type=jnp.float32)
        placed = placed.astype(bf16)
        for g in range(auxb // 4):
            parts = [placed[h * chunk:(h + 1) * chunk] for h in (2 * g, 2 * g + 1)]
            lanes = slice(g * 128, (g + 1) * 128)
            for q in range(4):
                piece = jnp.concatenate([part[:, q * 64:(q + 1) * 64] for part in parts], axis=1)
                if q == 0:
                    low_ref[0, rows, lanes] = jnp.where(first, piece, zero)
                    top_ref[1, rows, lanes] = jnp.where(first, zero, piece)
                    continue
                if q == 3:
                    top_ref[0, rows, lanes] = piece
                else:
                    mid_ref[q - 1, rows, lanes] = piece
                    low_ref[q, rows, lanes] = piece


def align(slabs, start, count):
    rows, auxb, _ = slabs.shape
    depth = auxb * 32
    bf16 = jnp.bfloat16
    return pl.pallas_call(
        functools.partial(align_kernel, CHUNKS),
        in_specs=[spec(SMEM)] * 2 + [spec(pl.ANY)],
        out_specs=[spec(VMEM)] * 3,
        out_shape=[jax.ShapeDtypeStruct((groups, rows, depth), bf16) for groups in (2, 2, 3)],
        scratch_shapes=[
            VMEM(slabs.shape, bf16),
            VMEM((256, 256), bf16),
            pltpu.SemaphoreType.DMA((len(CHUNKS),)),
        ],
        compiler_params=pltpu.CompilerParams(vmem_limit_bytes=49 * MIB),
    )(start, count, slabs)


def product(left, right):
    total = None
    for a, b in zip(left, right):
        term = lax.dot_general(a, b, NT, preferred_element_type=jnp.float32)
        total = term if total is None else total + term
    return total


def tile_sums(tile, place, weights_ref):
    parts = []
    for which in range(2):
        total = jnp.zeros((8, 256), jnp.float32)
        for source in range(4):
            weight = weights_ref[source, place * 2 + which].astype(jnp.float32)
            piece = weight * tile[source * 64:(source + 1) * 64]
            total = total + jnp.sum(piece.reshape(8, 8, 256), axis=0)
        parts.append(total)
    return parts


def own_kernel(row_ref, density_ref, direction_ref, mid_ref, top_ref, low_ref, local_ref, odd_ref, even_ref):
    block = row_ref[0, 0]
    for k in range(4):
        for which, source in enumerate((density_ref, direction_ref)):
            total = jnp.zeros(source.shape[2:], jnp.float32)
            for s in range(4):
                other = row_ref[0, s]
                full = 1.0 if s == 0 else 2.0
                weight = jnp.where((other >= 0) & (other - block == k), full, 0.0)
                total = total + weight * source[0, s].astype(jnp.float32)
            total = total.astype(jnp.bfloat16)
            if k == 0:
                local_ref[which] = total
                continue
            for to in range(4):
                if k == 2:
                    even_ref[to, which] = total
                else:
                    odd_ref[to, k // 2 * 2 + which] = total
    own = [low_ref[0], mid_ref[0], mid_ref[1], top_ref[0], top_ref[1]]
    tile = product(own, own)
    high = tile.astype(jnp.bfloat16)
    rest = (tile - high.astype(jnp.float32)).astype(jnp.bfloat16)
    for to in range(4):
        part = slice(to * 64, (to + 1) * 64)
        even_ref[to, 2] = high[part]
        even_ref[to, 3] = rest[part]


def near_kernel(mid_ref, top_ref, low_ref, before_mid_ref, before_top_ref, even_ref, local_ref, out_ref, own_ref, sums_ref):
    own = [low_ref[0], mid_ref[0], mid_ref[1], top_ref[0]]
    before = [before_mid_ref[0], before_mid_ref[1], before_top_ref[0], before_top_ref[1]]
    out_ref[...] = product(before, own)
    total = even_ref[0, 2].astype(jnp.float32) + even_ref[0, 3].astype(jnp.float32)
    for source in range(1, 4):
        total = total + even_ref[source, 2].astype(jnp.float32) + even_ref[source, 3].astype(jnp.float32)
    own_ref[...] = total.astype(jnp.bfloat16)
    for which in range(2):
        sums_ref[which] = jnp.sum((local_ref[which].astype(jnp.float32) * total).reshape(8, 8, 256), axis=0)


def far_kernel(mid_ref, top_ref, before_ref, after_ref, even_ref, odd_ref, near_ref, sums_in_ref, out_ref):
    after = [after_ref[q] for q in range(3)]
    t2 = product([mid_ref[1], top_ref[0], top_ref[1]], after)
    t3 = product([before_ref[q] for q in range(2)], after)
    sums = [sums_in_ref[0], sums_in_ref[1]]
    for tile, place, weights_ref in ((near_ref, 0, odd_ref), (t2, 0, even_ref), (t3, 1, odd_ref)):
        sums = [a + b for a, b in zip(sums, tile_sums(tile, place, weights_ref))]
    for to in range(4):
        part = slice(to * 64, (to + 1) * 64)
        for n, tile in enumerate((near_ref[part], t3[part], t2[part])):
            out_ref[to, n * 64:(n + 1) * 64] = tile.astype(jnp.bfloat16)
    lines = []
    for total in sums:
        value = jnp.broadcast_to(jnp.sum(total, keepdims=True), (8, 256))
        high = value.astype(jnp.bfloat16).astype(jnp.float32)
        rest = value - high
        middle = rest.astype(jnp.bfloat16).astype(jnp.float32)
        lines.append((high, middle, rest - middle))
    line = lax.broadcasted_iota(jnp.int32, (16, 256), 0)
    block = jnp.zeros((16, 256), jnp.float32)
    for which in range(2):
        for part in range(3):
            twice = jnp.concatenate([lines[which][part]] * 2, axis=0)
            block = jnp.where(line == which * 3 + part, twice, block)
    for to in range(4):
        out_ref[to, 192:208] = block.astype(jnp.bfloat16)


def sum_kernel(parts_ref, before_ref, own_ref, energy_ref):
    for n in range(3):
        rows = slice(n * 64, (n + 1) * 64)
        total = parts_ref[0, rows].astype(jnp.float32)
        for source in range(1, 4):
            total = total + parts_ref[source, rows].astype(jnp.float32)
        if n < 2:
            before_ref[n] = total.astype(jnp.bfloat16)
        else:
            own_ref[...] = total.astype(jnp.bfloat16)
    extra = parts_ref[0, 192:208].astype(jnp.float32)
    for source in range(1, 4):
        extra = extra + parts_ref[source, 192:208].astype(jnp.float32)
    first = extra[0:1] + extra[1:2] + extra[2:3]
    second = extra[3:4] + extra[4:5] + extra[5:6]
    lane = lax.broadcasted_iota(jnp.int32, (1, 128), 1)
    both = jnp.where(lane < 64, first[:, :128], second[:, :128])
    energy_ref[...] = jnp.broadcast_to(both[None], energy_ref.shape)


def finish_kernel(scale, row_ref, steps_ref, t0_ref, t2_ref, odd_ref, energy_ref, tiles_ref, out_ref):
    block = row_ref[0, 0]
    tiles = [t0_ref[...], odd_ref[0], t2_ref[...], odd_ref[1]]
    for s in range(4):
        other = row_ref[0, s]
        total = jnp.zeros(t0_ref.shape, jnp.float32)
        for k in range(4):
            chosen = (other >= 0) & (other - block == k)
            total = jnp.where(chosen, tiles[k].astype(jnp.float32), total)
        tiles_ref[0, s] = total.astype(jnp.bfloat16)
    total = jnp.sum(energy_ref[...], axis=0)
    first, second = total[:, :3], total[:, 64:67]
    out_ref[...] = -0.5 * (first + steps_ref[...] * second) * scale


def kernel_call(kernel, in_specs, out_shape, limit=16, out_specs=None):
    return pl.pallas_call(
        kernel,
        in_specs=in_specs,
        out_specs=out_specs or [spec(VMEM)] * len(out_shape),
        out_shape=out_shape,
        compiler_params=pltpu.CompilerParams(vmem_limit_bytes=limit * MIB),
    )


def body(slabs, orbital_start, orbital_count, partners, density, direction, step_lengths):
    rows = slabs.shape[0]
    aux = lax.axis_size("aux")
    blocks = lax.axis_size("blk")
    slots = partners.shape[1]
    part = rows // aux

    def half(*shape):
        return jax.ShapeDtypeStruct(shape, jnp.bfloat16)

    def single(*shape):
        return jax.ShapeDtypeStruct(shape, jnp.float32)

    mid, top, low = align(slabs, orbital_start, orbital_count)
    after = moved_by(low, "blk", -2)
    before_mid = moved_by(mid, "blk", 1)
    before_top = moved_by(top, "blk", 1)
    local, odd, even = kernel_call(
        own_kernel,
        [spec(SMEM)] + [spec(VMEM)] * 5,
        [half(2, part, rows), half(aux, 4, part, rows), half(aux, 4, part, rows)],
    )(partners, density, direction, mid, top, low)
    odd = lax.all_to_all(odd, "aux", 0, 0, tiled=True)
    odd = moved_by(odd, "blk", 1)

    even = lax.all_to_all(even, "aux", 0, 0, tiled=True)
    t1, t0, sums = kernel_call(
        near_kernel, [spec(VMEM)] * 7, [single(rows, rows), half(part, rows), single(2, 8, rows)]
    )(mid, top, low, before_mid, before_top, even, local)
    (far,) = kernel_call(far_kernel, [spec(VMEM)] * 8, [half(aux, 3 * part + 16, rows)])(
        mid, top, before_top, after, even, odd, t1, sums
    )
    far = lax.all_to_all(far, "aux", 0, 0, tiled=True)
    odd, t2, energy = kernel_call(
        sum_kernel, [spec(VMEM)], [half(2, part, rows), half(part, rows), single(blocks, 1, 128)]
    )(far)
    odd = moved_by(odd, "blk", -1)
    energy = lax.all_to_all(energy, "blk", 0, 0, tiled=True)

    scale = 1.0 / (rows * math.sqrt(blocks * slots))
    tiles, energies = kernel_call(
        functools.partial(finish_kernel, scale),
        [spec(SMEM)] + [spec(VMEM)] * 5,
        [half(1, slots, part, rows), single(1, 3)],
    )(partners, step_lengths[None], t0, t2, odd, energy)
    return tiles, energies[0]


def solution(mesh):
    return jax.shard_map(
        body,
        mesh=mesh,
        in_specs=(
            P("blk", "aux", None),
            P("blk"),
            P("blk"),
            P("blk", None),
            P("blk", None, "aux", None),
            P("blk", None, "aux", None),
            P(),
        ),
        out_specs=(P("blk", None, "aux", None), P()),
        check_vma=False,
    )
```

```python
import functools
import math

import jax
import jax.numpy as jnp
from jax import lax
from jax.experimental import pallas as pl
from jax.experimental.pallas import tpu as pltpu
from jax.sharding import PartitionSpec as P

VMEM = pltpu.VMEM
SMEM = pltpu.SMEM
NT = (((1,), (1,)), ((), ()))
MIB = 1024 * 1024
CHUNKS = (64, 96, 96)


def spec(space):
    return pl.BlockSpec(memory_space=space)


def moved_by(value, axis, steps):
    count = lax.axis_size(axis)
    pairs = [(source, source + steps) for source in range(count) if 0 <= source + steps < count]
    return lax.ppermute(value, axis, pairs)


def align_kernel(
    chunks, start_ref, count_ref, slab_hbm, mid_ref, top_ref, low_ref, slab_ref, select_ref, sem
):
    _, auxb, _ = slab_ref.shape
    bf16 = jnp.bfloat16
    begins = [sum(chunks[:n]) for n in range(len(chunks))]
    loads = [
        pltpu.make_async_copy(slab_hbm.at[pl.ds(begin, chunk)], slab_ref.at[pl.ds(begin, chunk)], sem.at[n])
        for n, (begin, chunk) in enumerate(zip(begins, chunks))
    ]
    for copy in loads:
        copy.start()
    shift = start_ref[0] & 31
    count = count_ref[0]
    a = lax.broadcasted_iota(jnp.int32, (128, 256), 0)
    to = lax.broadcasted_iota(jnp.int32, (128, 256), 1)
    hit = (a < count) & (((a + shift) & 127) == ((to >> 6) << 5) + (to & 31))
    for m in range(2):
        select_ref[m * 128:(m + 1) * 128] = jnp.where(hit & (((to >> 5) & 1) == m), 1.0, 0.0).astype(bf16)
    for load, begin, chunk in zip(loads, begins, chunks):
        first = (lax.broadcasted_iota(jnp.int32, (chunk, 128), 1) & 31) >= shift
        zero = jnp.zeros((chunk, 128), bf16)
        rows = slice(begin, begin + chunk)
        load.wait()
        by_function = jnp.swapaxes(slab_ref[rows], 0, 1)
        pairs = [jnp.concatenate([by_function[p], by_function[p + 1]], axis=1) for p in range(0, auxb, 2)]
        placed = jnp.dot(jnp.concatenate(pairs, axis=0), select_ref[...], preferred_element_type=jnp.float32)
        placed = placed.astype(bf16)
        for g in range(auxb // 4):
            parts = [placed[h * chunk:(h + 1) * chunk] for h in (2 * g, 2 * g + 1)]
            lanes = slice(g * 128, (g + 1) * 128)
            for q in range(4):
                piece = jnp.concatenate([part[:, q * 64:(q + 1) * 64] for part in parts], axis=1)
                if q == 0:
                    low_ref[0, rows, lanes] = jnp.where(first, piece, zero)
                    top_ref[1, rows, lanes] = jnp.where(first, zero, piece)
                    continue
                if q == 3:
                    top_ref[0, rows, lanes] = piece
                else:
                    mid_ref[q - 1, rows, lanes] = piece
                    low_ref[q, rows, lanes] = piece


def align(slabs, start, count):
    rows, auxb, _ = slabs.shape
    depth = auxb * 32
    bf16 = jnp.bfloat16
    return pl.pallas_call(
        functools.partial(align_kernel, CHUNKS),
        in_specs=[spec(SMEM)] * 2 + [spec(pl.ANY)],
        out_specs=[spec(VMEM)] * 3,
        out_shape=[jax.ShapeDtypeStruct((groups, rows, depth), bf16) for groups in (2, 2, 3)],
        scratch_shapes=[
            VMEM(slabs.shape, bf16),
            VMEM((256, 256), bf16),
            pltpu.SemaphoreType.DMA((len(CHUNKS),)),
        ],
        compiler_params=pltpu.CompilerParams(vmem_limit_bytes=49 * MIB),
    )(start, count, slabs)


def product(left, right):
    total = None
    for a, b in zip(left, right):
        term = lax.dot_general(a, b, NT, preferred_element_type=jnp.float32)
        total = term if total is None else total + term
    return total


def tile_sums(tile, place, weights_ref):
    parts = []
    for which in range(2):
        total = jnp.zeros((8, 256), jnp.float32)
        for source in range(4):
            weight = weights_ref[source, place * 2 + which].astype(jnp.float32)
            piece = weight * tile[source * 64:(source + 1) * 64]
            total = total + jnp.sum(piece.reshape(8, 8, 256), axis=0)
        parts.append(total)
    return parts


def own_kernel(row_ref, density_ref, direction_ref, mid_ref, top_ref, low_ref, local_ref, odd_ref, even_ref):
    block = row_ref[0, 0]
    for k in range(4):
        for which, source in enumerate((density_ref, direction_ref)):
            total = jnp.zeros(source.shape[2:], jnp.float32)
            for s in range(4):
                other = row_ref[0, s]
                full = 1.0 if s == 0 else 2.0
                weight = jnp.where((other >= 0) & (other - block == k), full, 0.0)
                total = total + weight * source[0, s].astype(jnp.float32)
            total = total.astype(jnp.bfloat16)
            if k == 0:
                local_ref[which] = total
                continue
            for to in range(4):
                if k == 2:
                    even_ref[to, which] = total
                else:
                    odd_ref[to, k // 2 * 2 + which] = total
    own = [low_ref[0], mid_ref[0], mid_ref[1], top_ref[0], top_ref[1]]
    tile = product(own, own)
    high = tile.astype(jnp.bfloat16)
    rest = (tile - high.astype(jnp.float32)).astype(jnp.bfloat16)
    for to in range(4):
        part = slice(to * 64, (to + 1) * 64)
        even_ref[to, 2] = high[part]
        even_ref[to, 3] = rest[part]


def near_kernel(mid_ref, top_ref, low_ref, before_mid_ref, before_top_ref, even_ref, local_ref, out_ref, own_ref, sums_ref):
    own = [low_ref[0], mid_ref[0], mid_ref[1], top_ref[0]]
    before = [before_mid_ref[0], before_mid_ref[1], before_top_ref[0], before_top_ref[1]]
    out_ref[...] = product(before, own)
    total = even_ref[0, 2].astype(jnp.float32) + even_ref[0, 3].astype(jnp.float32)
    for source in range(1, 4):
        total = total + even_ref[source, 2].astype(jnp.float32) + even_ref[source, 3].astype(jnp.float32)
    own_ref[...] = total.astype(jnp.bfloat16)
    for which in range(2):
        sums_ref[which] = jnp.sum((local_ref[which].astype(jnp.float32) * total).reshape(8, 8, 256), axis=0)


def far_kernel(mid_ref, top_ref, before_ref, after_ref, even_ref, odd_ref, near_ref, sums_in_ref, out_ref):
    after = [after_ref[q] for q in range(3)]
    t2 = product([mid_ref[1], top_ref[0], top_ref[1]], after)
    t3 = product([before_ref[q] for q in range(2)], after)
    sums = [sums_in_ref[0], sums_in_ref[1]]
    for tile, place, weights_ref in ((near_ref, 0, odd_ref), (t2, 0, even_ref), (t3, 1, odd_ref)):
        sums = [a + b for a, b in zip(sums, tile_sums(tile, place, weights_ref))]
    for to in range(4):
        part = slice(to * 64, (to + 1) * 64)
        for n, tile in enumerate((near_ref[part], t3[part], t2[part])):
            out_ref[to, n * 64:(n + 1) * 64] = tile.astype(jnp.bfloat16)
    lines = []
    for total in sums:
        value = jnp.broadcast_to(jnp.sum(total, keepdims=True), (8, 256))
        high = value.astype(jnp.bfloat16).astype(jnp.float32)
        rest = value - high
        middle = rest.astype(jnp.bfloat16).astype(jnp.float32)
        lines.append((high, middle, rest - middle))
    line = lax.broadcasted_iota(jnp.int32, (16, 256), 0)
    block = jnp.zeros((16, 256), jnp.float32)
    for which in range(2):
        for part in range(3):
            twice = jnp.concatenate([lines[which][part]] * 2, axis=0)
            block = jnp.where(line == which * 3 + part, twice, block)
    for to in range(4):
        out_ref[to, 192:208] = block.astype(jnp.bfloat16)


def sum_kernel(parts_ref, before_ref, own_ref, energy_ref):
    for n in range(3):
        rows = slice(n * 64, (n + 1) * 64)
        total = parts_ref[0, rows].astype(jnp.float32)
        for source in range(1, 4):
            total = total + parts_ref[source, rows].astype(jnp.float32)
        if n < 2:
            before_ref[n] = total.astype(jnp.bfloat16)
        else:
            own_ref[...] = total.astype(jnp.bfloat16)
    extra = parts_ref[0, 192:208].astype(jnp.float32)
    for source in range(1, 4):
        extra = extra + parts_ref[source, 192:208].astype(jnp.float32)
    first = extra[0:1] + extra[1:2] + extra[2:3]
    second = extra[3:4] + extra[4:5] + extra[5:6]
    lane = lax.broadcasted_iota(jnp.int32, (1, 128), 1)
    both = jnp.where(lane < 64, first[:, :128], second[:, :128])
    energy_ref[...] = jnp.broadcast_to(both[None], energy_ref.shape)


def finish_kernel(scale, row_ref, steps_ref, t0_ref, t2_ref, odd_ref, energy_ref, tiles_hbm, out_ref, tiles_ref, sem):
    block = row_ref[0, 0]
    tiles = [t0_ref[...], odd_ref[0], t2_ref[...], odd_ref[1]]
    for s in range(4):
        other = row_ref[0, s]
        total = jnp.zeros(t0_ref.shape, jnp.float32)
        for k in range(4):
            chosen = (other >= 0) & (other - block == k)
            total = jnp.where(chosen, tiles[k].astype(jnp.float32), total)
        tiles_ref[0, s] = total.astype(jnp.bfloat16)
    copy = pltpu.make_async_copy(tiles_ref, tiles_hbm, sem)
    copy.start()
    total = jnp.sum(energy_ref[...], axis=0)
    first, second = total[:, :3], total[:, 64:67]
    out_ref[...] = -0.5 * (first + steps_ref[...] * second) * scale
    copy.wait()


def kernel_call(kernel, in_specs, out_shape, limit=16, out_specs=None, scratch=()):
    return pl.pallas_call(
        kernel,
        in_specs=in_specs,
        out_specs=out_specs or [spec(VMEM)] * len(out_shape),
        out_shape=out_shape,
        scratch_shapes=list(scratch),
        compiler_params=pltpu.CompilerParams(vmem_limit_bytes=limit * MIB),
    )


def body(slabs, orbital_start, orbital_count, partners, density, direction, step_lengths):
    rows = slabs.shape[0]
    aux = lax.axis_size("aux")
    blocks = lax.axis_size("blk")
    slots = partners.shape[1]
    part = rows // aux

    def half(*shape):
        return jax.ShapeDtypeStruct(shape, jnp.bfloat16)

    def single(*shape):
        return jax.ShapeDtypeStruct(shape, jnp.float32)

    mid, top, low = align(slabs, orbital_start, orbital_count)
    after = moved_by(low, "blk", -2)
    before_mid = moved_by(mid, "blk", 1)
    before_top = moved_by(top, "blk", 1)
    local, odd, even = kernel_call(
        own_kernel,
        [spec(SMEM)] + [spec(VMEM)] * 5,
        [half(2, part, rows), half(aux, 4, part, rows), half(aux, 4, part, rows)],
    )(partners, density, direction, mid, top, low)
    odd = lax.all_to_all(odd, "aux", 0, 0, tiled=True)
    odd = moved_by(odd, "blk", 1)

    even = lax.all_to_all(even, "aux", 0, 0, tiled=True)
    t1, t0, sums = kernel_call(
        near_kernel, [spec(VMEM)] * 7, [single(rows, rows), half(part, rows), single(2, 8, rows)]
    )(mid, top, low, before_mid, before_top, even, local)
    (far,) = kernel_call(far_kernel, [spec(VMEM)] * 8, [half(aux, 3 * part + 16, rows)])(
        mid, top, before_top, after, even, odd, t1, sums
    )
    far = lax.all_to_all(far, "aux", 0, 0, tiled=True)
    odd, t2, energy = kernel_call(
        sum_kernel, [spec(VMEM)], [half(2, part, rows), half(part, rows), single(blocks, 1, 128)]
    )(far)
    odd = moved_by(odd, "blk", -1)
    energy = lax.all_to_all(energy, "blk", 0, 0, tiled=True)

    scale = 1.0 / (rows * math.sqrt(blocks * slots))
    tiles, energies = kernel_call(
        functools.partial(finish_kernel, scale),
        [spec(SMEM)] + [spec(VMEM)] * 5,
        [half(1, slots, part, rows), single(1, 3)],
        out_specs=[spec(pl.ANY), spec(VMEM)],
        scratch=[VMEM((1, slots, part, rows), jnp.bfloat16), pltpu.SemaphoreType.DMA(())],
    )(partners, step_lengths[None], t0, t2, odd, energy)
    return tiles, energies[0]


def solution(mesh):
    return jax.shard_map(
        body,
        mesh=mesh,
        in_specs=(
            P("blk", "aux", None),
            P("blk"),
            P("blk"),
            P("blk", None),
            P("blk", None, "aux", None),
            P("blk", None, "aux", None),
            P(),
        ),
        out_specs=(P("blk", None, "aux", None), P()),
        check_vma=False,
    )
```

```python
import functools
import math

import jax
import jax.numpy as jnp
from jax import lax
from jax.experimental import pallas as pl
from jax.experimental.pallas import tpu as pltpu
from jax.sharding import PartitionSpec as P

VMEM = pltpu.VMEM
SMEM = pltpu.SMEM
NT = (((1,), (1,)), ((), ()))
MIB = 1024 * 1024
CHUNKS = (32, 96, 128)


def spec(space):
    return pl.BlockSpec(memory_space=space)


def moved_by(value, axis, steps):
    count = lax.axis_size(axis)
    pairs = [(source, source + steps) for source in range(count) if 0 <= source + steps < count]
    return lax.ppermute(value, axis, pairs)


def align_kernel(
    chunks, start_ref, count_ref, slab_hbm, mid_ref, top_ref, low_ref, slab_ref, select_ref, sem
):
    _, auxb, _ = slab_ref.shape
    bf16 = jnp.bfloat16
    begins = [sum(chunks[:n]) for n in range(len(chunks))]
    loads = [
        pltpu.make_async_copy(slab_hbm.at[pl.ds(begin, chunk)], slab_ref.at[pl.ds(begin, chunk)], sem.at[n])
        for n, (begin, chunk) in enumerate(zip(begins, chunks))
    ]
    for copy in loads:
        copy.start()
    shift = start_ref[0] & 31
    count = count_ref[0]
    a = lax.broadcasted_iota(jnp.int32, (128, 256), 0)
    to = lax.broadcasted_iota(jnp.int32, (128, 256), 1)
    hit = (a < count) & (((a + shift) & 127) == ((to >> 6) << 5) + (to & 31))
    for m in range(2):
        select_ref[m * 128:(m + 1) * 128] = jnp.where(hit & (((to >> 5) & 1) == m), 1.0, 0.0).astype(bf16)
    for load, begin, chunk in zip(loads, begins, chunks):
        first = (lax.broadcasted_iota(jnp.int32, (chunk, 128), 1) & 31) >= shift
        zero = jnp.zeros((chunk, 128), bf16)
        rows = slice(begin, begin + chunk)
        load.wait()
        by_function = jnp.swapaxes(slab_ref[rows], 0, 1)
        pairs = [jnp.concatenate([by_function[p], by_function[p + 1]], axis=1) for p in range(0, auxb, 2)]
        placed = jnp.dot(jnp.concatenate(pairs, axis=0), select_ref[...], preferred_element_type=jnp.float32)
        placed = placed.astype(bf16)
        for g in range(auxb // 4):
            parts = [placed[h * chunk:(h + 1) * chunk] for h in (2 * g, 2 * g + 1)]
            lanes = slice(g * 128, (g + 1) * 128)
            for q in range(4):
                piece = jnp.concatenate([part[:, q * 64:(q + 1) * 64] for part in parts], axis=1)
                if q == 0:
                    low_ref[0, rows, lanes] = jnp.where(first, piece, zero)
                    top_ref[1, rows, lanes] = jnp.where(first, zero, piece)
                    continue
                if q == 3:
                    top_ref[0, rows, lanes] = piece
                else:
                    mid_ref[q - 1, rows, lanes] = piece
                    low_ref[q, rows, lanes] = piece


def align(slabs, start, count):
    rows, auxb, _ = slabs.shape
    depth = auxb * 32
    bf16 = jnp.bfloat16
    return pl.pallas_call(
        functools.partial(align_kernel, CHUNKS),
        in_specs=[spec(SMEM)] * 2 + [spec(pl.ANY)],
        out_specs=[spec(VMEM)] * 3,
        out_shape=[jax.ShapeDtypeStruct((groups, rows, depth), bf16) for groups in (2, 2, 3)],
        scratch_shapes=[
            VMEM(slabs.shape, bf16),
            VMEM((256, 256), bf16),
            pltpu.SemaphoreType.DMA((len(CHUNKS),)),
        ],
        compiler_params=pltpu.CompilerParams(vmem_limit_bytes=49 * MIB),
    )(start, count, slabs)


def by_offset_kernel(row_ref, density_ref, direction_ref, even_ref, odd_ref):
    block = row_ref[0, 0]
    for k in range(4):
        for which, source in enumerate((density_ref, direction_ref)):
            total = jnp.zeros(source.shape[2:], jnp.float32)
            for s in range(4):
                other = row_ref[0, s]
                full = 1.0 if s == 0 else 2.0
                weight = jnp.where((other >= 0) & (other - block == k), full, 0.0)
                total = total + weight * source[0, s].astype(jnp.float32)
            total = total.astype(jnp.bfloat16)
            if k % 2 == 0:
                even_ref[k // 2 * 2 + which] = total
            else:
                for to in range(4):
                    odd_ref[to, k // 2 * 2 + which] = total


def product(left, right):
    total = None
    for a, b in zip(left, right):
        term = lax.dot_general(a, b, NT, preferred_element_type=jnp.float32)
        total = term if total is None else total + term
    return total


def tile_sums(tile, place, weights_ref):
    parts = []
    for which in range(2):
        total = jnp.zeros((8, 256), jnp.float32)
        for source in range(4):
            weight = weights_ref[source, place * 2 + which].astype(jnp.float32)
            piece = weight * tile[source * 64:(source + 1) * 64]
            total = total + jnp.sum(piece.reshape(8, 8, 256), axis=0)
        parts.append(total)
    return parts


def own_kernel(mid_ref, top_ref, low_ref, even_ref, out_ref):
    own = [low_ref[0], mid_ref[0], mid_ref[1], top_ref[0], top_ref[1]]
    tile = product(own, own)
    high = tile.astype(jnp.bfloat16)
    rest = (tile - high.astype(jnp.float32)).astype(jnp.bfloat16)
    for to in range(4):
        part = slice(to * 64, (to + 1) * 64)
        out_ref[to, 0] = even_ref[2]
        out_ref[to, 1] = even_ref[3]
        out_ref[to, 2] = high[part]
        out_ref[to, 3] = rest[part]


def near_kernel(mid_ref, top_ref, low_ref, before_mid_ref, before_top_ref, even_ref, local_ref, out_ref, own_ref, sums_ref):
    own = [low_ref[0], mid_ref[0], mid_ref[1], top_ref[0]]
    before = [before_mid_ref[0], before_mid_ref[1], before_top_ref[0], before_top_ref[1]]
    out_ref[...] = product(before, own)
    total = even_ref[0, 2].astype(jnp.float32) + even_ref[0, 3].astype(jnp.float32)
    for source in range(1, 4):
        total = total + even_ref[source, 2].astype(jnp.float32) + even_ref[source, 3].astype(jnp.float32)
    own_ref[...] = total.astype(jnp.bfloat16)
    for which in range(2):
        sums_ref[which] = jnp.sum((local_ref[which].astype(jnp.float32) * total).reshape(8, 8, 256), axis=0)


def far_kernel(mid_ref, top_ref, before_ref, after_ref, even_ref, odd_ref, near_ref, sums_in_ref, out_ref):
    after = [after_ref[q] for q in range(3)]
    t2 = product([mid_ref[1], top_ref[0], top_ref[1]], after)
    t3 = product([before_ref[q] for q in range(2)], after)
    sums = [sums_in_ref[0], sums_in_ref[1]]
    for tile, place, weights_ref in ((near_ref, 0, odd_ref), (t2, 0, even_ref), (t3, 1, odd_ref)):
        sums = [a + b for a, b in zip(sums, tile_sums(tile, place, weights_ref))]
    for to in range(4):
        part = slice(to * 64, (to + 1) * 64)
        for n, tile in enumerate((near_ref[part], t3[part], t2[part])):
            out_ref[to, n * 64:(n + 1) * 64] = tile.astype(jnp.bfloat16)
    lines = []
    for total in sums:
        value = jnp.broadcast_to(jnp.sum(total, keepdims=True), (8, 256))
        high = value.astype(jnp.bfloat16).astype(jnp.float32)
        rest = value - high
        middle = rest.astype(jnp.bfloat16).astype(jnp.float32)
        lines.append((high, middle, rest - middle))
    line = lax.broadcasted_iota(jnp.int32, (16, 256), 0)
    block = jnp.zeros((16, 256), jnp.float32)
    for which in range(2):
        for part in range(3):
            twice = jnp.concatenate([lines[which][part]] * 2, axis=0)
            block = jnp.where(line == which * 3 + part, twice, block)
    for to in range(4):
        out_ref[to, 192:208] = block.astype(jnp.bfloat16)


def sum_kernel(parts_ref, before_ref, own_ref, energy_ref):
    for n in range(3):
        rows = slice(n * 64, (n + 1) * 64)
        total = parts_ref[0, rows].astype(jnp.float32)
        for source in range(1, 4):
            total = total + parts_ref[source, rows].astype(jnp.float32)
        if n < 2:
            before_ref[n] = total.astype(jnp.bfloat16)
        else:
            own_ref[...] = total.astype(jnp.bfloat16)
    extra = parts_ref[0, 192:208].astype(jnp.float32)
    for source in range(1, 4):
        extra = extra + parts_ref[source, 192:208].astype(jnp.float32)
    first = extra[0:1] + extra[1:2] + extra[2:3]
    second = extra[3:4] + extra[4:5] + extra[5:6]
    lane = lax.broadcasted_iota(jnp.int32, (1, 128), 1)
    both = jnp.where(lane < 64, first[:, :128], second[:, :128])
    energy_ref[...] = jnp.broadcast_to(both[None], energy_ref.shape)


def finish_kernel(scale, row_ref, steps_ref, t0_ref, t2_ref, odd_ref, energy_ref, tiles_ref, out_ref):
    block = row_ref[0, 0]
    tiles = [t0_ref[...], odd_ref[0], t2_ref[...], odd_ref[1]]
    for s in range(4):
        other = row_ref[0, s]
        total = jnp.zeros(t0_ref.shape, jnp.float32)
        for k in range(4):
            chosen = (other >= 0) & (other - block == k)
            total = jnp.where(chosen, tiles[k].astype(jnp.float32), total)
        tiles_ref[0, s] = total.astype(jnp.bfloat16)
    total = jnp.sum(energy_ref[...], axis=0)
    first, second = total[:, :3], total[:, 64:67]
    out_ref[...] = -0.5 * (first + steps_ref[...] * second) * scale


def kernel_call(kernel, in_specs, out_shape, limit=16, out_specs=None):
    return pl.pallas_call(
        kernel,
        in_specs=in_specs,
        out_specs=out_specs or [spec(VMEM)] * len(out_shape),
        out_shape=out_shape,
        compiler_params=pltpu.CompilerParams(vmem_limit_bytes=limit * MIB),
    )


def body(slabs, orbital_start, orbital_count, partners, density, direction, step_lengths):
    rows = slabs.shape[0]
    aux = lax.axis_size("aux")
    blocks = lax.axis_size("blk")
    slots = partners.shape[1]
    part = rows // aux

    def half(*shape):
        return jax.ShapeDtypeStruct(shape, jnp.bfloat16)

    def single(*shape):
        return jax.ShapeDtypeStruct(shape, jnp.float32)

    mid, top, low = align(slabs, orbital_start, orbital_count)
    after = moved_by(low, "blk", -2)
    before_mid = moved_by(mid, "blk", 1)
    before_top = moved_by(top, "blk", 1)
    low, density, direction = lax.optimization_barrier((low, density, direction))
    even, odd = kernel_call(by_offset_kernel, [spec(SMEM)] + [spec(VMEM)] * 2, [half(4, part, rows), half(aux, 4, part, rows)])(
        partners, density, direction
    )
    odd = lax.all_to_all(odd, "aux", 0, 0, tiled=True)
    odd = moved_by(odd, "blk", 1)

    local = even
    (even,) = kernel_call(own_kernel, [spec(VMEM)] * 4, [half(aux, 4, part, rows)])(mid, top, low, local)
    even = lax.all_to_all(even, "aux", 0, 0, tiled=True)
    t1, t0, sums = kernel_call(
        near_kernel, [spec(VMEM)] * 7, [single(rows, rows), half(part, rows), single(2, 8, rows)]
    )(mid, top, low, before_mid, before_top, even, local)
    (far,) = kernel_call(far_kernel, [spec(VMEM)] * 8, [half(aux, 3 * part + 16, rows)])(
        mid, top, before_top, after, even, odd, t1, sums
    )
    far = lax.all_to_all(far, "aux", 0, 0, tiled=True)
    odd, t2, energy = kernel_call(
        sum_kernel, [spec(VMEM)], [half(2, part, rows), half(part, rows), single(blocks, 1, 128)]
    )(far)
    odd = moved_by(odd, "blk", -1)
    energy = lax.all_to_all(energy, "blk", 0, 0, tiled=True)

    scale = 1.0 / (rows * math.sqrt(blocks * slots))
    tiles, energies = kernel_call(
        functools.partial(finish_kernel, scale),
        [spec(SMEM)] + [spec(VMEM)] * 5,
        [half(1, slots, part, rows), single(1, 3)],
    )(partners, step_lengths[None], t0, t2, odd, energy)
    return tiles, energies[0]


def solution(mesh):
    return jax.shard_map(
        body,
        mesh=mesh,
        in_specs=(
            P("blk", "aux", None),
            P("blk"),
            P("blk"),
            P("blk", None),
            P("blk", None, "aux", None),
            P("blk", None, "aux", None),
            P(),
        ),
        out_specs=(P("blk", None, "aux", None), P()),
        check_vma=False,
    )
```
